256 devices in a mesh: resp: 8 (over x, y_hi), blk: 32 (over z, y_lo, core).
Axes of the slice: x: 4, y: 4 (y_hi: 2, y_lo: 2; y = y_hi * 2 + y_lo), z: 8, core: 2. Of those that a mesh axis runs over, the one named last changes fastest.
Arguments:
- response_query: bfloat16 [8, 4096, 1792], P('resp', 'blk'), may hold values from -8 to 8
- response_key: bfloat16 [8, 4096, 256], P('resp', 'blk'), may hold values from -6 to 6
- response_value: bfloat16 [8, 4096, 256], P('resp', 'blk'), may hold values from -6 to 6
- shared_prompt_key: bfloat16 [2048, 256], P('blk'), may hold values from -8 to 8
- shared_prompt_value: bfloat16 [2048, 256], P('blk'), may hold values from -6 to 6
- grad_out: bfloat16 [8, 4096, 1792], P('resp', 'blk'), may hold values from -48 to 48
- lengths: int32 [8], P('resp'), may hold values from 128 to 4096, as said below
Outputs:
- grad_q: bfloat16 [8, 4096, 1792], P('resp', 'blk')
- grad_k_resp: bfloat16 [8, 4096, 256], P('resp', 'blk')
- grad_v_resp: bfloat16 [8, 4096, 256], P('resp', 'blk')
- prompt_key_gradient: bfloat16 [2048, 256], P('blk')
- prompt_value_gradient: bfloat16 [2048, 256], P('blk')
The draws below stay inside these ranges and needn't reach their ends.
Inputs may be any that keep to these rules, and one draw needn't show every extreme that they name: `lengths`: multiples of 128.
All inputs are finite; a program needn't handle non-finite values.
Results may differ from the reference program's by a relative error of at most 0.014.
Values may be sent and summed in bfloat16 or wider, within the bound.
A program may use at most 64 MiB of HBM per device.

```python
import jax
import jax.numpy as jnp
from jax import lax

QUERY_HEADS = 14
KEY_VALUE_HEADS = 2
HEAD_WIDTH = 128
R_DEV = 128
RESPONSE_COUNT = 8
RESPONSE_LENGTH = 4096
PROMPT_LENGTH = 2048


def draw_response_query(key, part):
    key = jax.random.fold_in(key, 3)
    return jnp.clip(jax.random.normal(key, (RESPONSE_COUNT, RESPONSE_LENGTH, QUERY_HEADS * HEAD_WIDTH), jnp.float32), -6.0, 6.0).astype(jnp.bfloat16)


def draw_shared_prompt_key(key, part):
    key = jax.random.fold_in(key, 7)
    return jnp.clip(jax.random.normal(key, (PROMPT_LENGTH, KEY_VALUE_HEADS * HEAD_WIDTH), jnp.float32), -6.0, 6.0).astype(jnp.bfloat16)


def draw_lengths(key, part):
    key = jax.random.fold_in(key, 9)
    key_units, key_full = jax.random.split(key)
    blocks_most = RESPONSE_LENGTH // R_DEV
    units = jax.random.randint(key_units, (RESPONSE_COUNT,), 1, blocks_most + 1)
    full_one = jax.random.randint(key_full, (), 0, RESPONSE_COUNT)
    units = jnp.where(jnp.arange(RESPONSE_COUNT) == full_one, blocks_most, units)
    return (units * R_DEV).astype(jnp.int32)


def levels(stream_key, extent, cuts, low, largest):
    gain, own = 1.0, jax.random.fold_in(stream_key, 6)
    for dim, shards_of in cuts:
        steps = jnp.exp(jax.random.uniform(jax.random.fold_in(own, dim), (shards_of,), jnp.float32, low / len(cuts), largest / len(cuts)))
        gain = gain * jnp.repeat(steps, extent[dim] // shards_of).reshape([-1 if axis == dim else 1 for axis in range(len(extent))])
    return gain


def normal_values(rng, extent, width, bound, shards=(), held_as=jnp.bfloat16):
    factor_of = levels(rng, extent, shards, -0.22, 0.18) if shards else 1.0
    array = jax.random.normal(rng, extent, jnp.float32) * width * factor_of
    return jnp.minimum(jnp.maximum(array, -bound), bound).astype(held_as)


def setup_inputs(seed: int = 0) -> dict:
    seeds = jax.random.split(jax.random.key(seed), 8)
    return {
        "response_query": draw_response_query(jax.random.fold_in(seeds[7], 71), 0),
        "response_key": normal_values(seeds[1], (RESPONSE_COUNT, RESPONSE_LENGTH, KEY_VALUE_HEADS * HEAD_WIDTH), 1.0, 6.0, ((0, 8), (1, 32))),
        "response_value": normal_values(seeds[2], (RESPONSE_COUNT, RESPONSE_LENGTH, KEY_VALUE_HEADS * HEAD_WIDTH), 1.0, 6.0, ((0, 8), (1, 32))),
        "shared_prompt_key": draw_shared_prompt_key(jax.random.fold_in(seeds[7], 71), 0),
        "shared_prompt_value": normal_values(seeds[4], (PROMPT_LENGTH, KEY_VALUE_HEADS * HEAD_WIDTH), 1.0, 6.0, ((0, 32),)),
        "grad_out": normal_values(seeds[5], (RESPONSE_COUNT, RESPONSE_LENGTH, QUERY_HEADS * HEAD_WIDTH), 8.0, 48.0, ((0, 8), (1, 32))),
        "lengths": draw_lengths(jax.random.fold_in(seeds[7], 71), 0),
    }


def reference(response_query, response_key, response_value, shared_prompt_key, shared_prompt_value, grad_out, lengths):
    group_width = QUERY_HEADS // KEY_VALUE_HEADS
    logit_scale = HEAD_WIDTH ** -0.5
    query_step = min(512, RESPONSE_LENGTH)
    steps_count = RESPONSE_LENGTH // query_step
    prompt_key_rows = shared_prompt_key.astype(jnp.float32).reshape(PROMPT_LENGTH, KEY_VALUE_HEADS, HEAD_WIDTH)
    prompt_value_rows = shared_prompt_value.astype(jnp.float32).reshape(PROMPT_LENGTH, KEY_VALUE_HEADS, HEAD_WIDTH)
    key_pos = jnp.concatenate([jnp.full((PROMPT_LENGTH,), -1, jnp.int32), jnp.arange(RESPONSE_LENGTH, dtype=jnp.int32)])

    def one_response(sums, inputs):
        query_rows, response_keys, response_values, gradient_list, resp_length = inputs
        positions = jnp.arange(RESPONSE_LENGTH, dtype=jnp.int32)
        gradient_list = jnp.where((positions < resp_length)[:, None], gradient_list, jnp.zeros_like(gradient_list))
        combined_queries = query_rows.astype(jnp.float32).reshape(RESPONSE_LENGTH, KEY_VALUE_HEADS, group_width, HEAD_WIDTH)
        gradient_combined = gradient_list.astype(jnp.float32).reshape(RESPONSE_LENGTH, KEY_VALUE_HEADS, group_width, HEAD_WIDTH)
        combined_keys = jnp.concatenate([prompt_key_rows, response_keys.astype(jnp.float32).reshape(RESPONSE_LENGTH, KEY_VALUE_HEADS, HEAD_WIDTH)], 0)
        combined_values = jnp.concatenate([prompt_value_rows, response_values.astype(jnp.float32).reshape(RESPONSE_LENGTH, KEY_VALUE_HEADS, HEAD_WIDTH)], 0)

        def one_block(totals, block_index):
            key_gradient, value_gradient = totals
            block_start = block_index * query_step
            query_block = lax.dynamic_slice_in_dim(combined_queries, block_start, query_step, 0)
            grad_block = lax.dynamic_slice_in_dim(gradient_combined, block_start, query_step, 0)
            query_pos = block_start + jnp.arange(query_step, dtype=jnp.int32)
            logits = jnp.einsum('tgjd,kgd->gjtk', query_block, combined_keys) * logit_scale
            visible = key_pos[None, :] <= query_pos[:, None]
            logits = jnp.where(visible, logits, -jnp.inf)
            row_top = jnp.max(logits, axis=-1, keepdims=True)
            row_total = jnp.sum(jnp.exp(logits - row_top), axis=-1, keepdims=True)
            weights = jnp.exp(logits - (row_top + jnp.log(row_total)))
            grad_prob = jnp.einsum('tgjd,kgd->gjtk', grad_block, combined_values)
            grad_dot = jnp.sum(weights * grad_prob, axis=-1, keepdims=True)
            grad_logit = lax.optimization_barrier((weights * (grad_prob - grad_dot)).astype(jnp.bfloat16)).astype(jnp.float32)
            weights_low = lax.optimization_barrier(weights.astype(jnp.bfloat16)).astype(jnp.float32)
            query_grad = jnp.einsum('gjtk,kgd->tgjd', grad_logit, combined_keys) * logit_scale
            key_gradient = key_gradient + jnp.einsum('gjtk,tgjd->kgd', grad_logit, query_block) * logit_scale
            value_gradient = value_gradient + jnp.einsum('gjtk,tgjd->kgd', weights_low, grad_block)
            return (key_gradient, value_gradient), query_grad

        blank_buffer = jnp.zeros((PROMPT_LENGTH + RESPONSE_LENGTH, KEY_VALUE_HEADS, HEAD_WIDTH), jnp.float32)
        (key_gradient, value_gradient), query_grads = lax.scan(one_block, (blank_buffer, blank_buffer), jnp.arange(steps_count, dtype=jnp.int32))
        grad_query = query_grads.reshape(RESPONSE_LENGTH, QUERY_HEADS * HEAD_WIDTH).astype(jnp.bfloat16)
        response_key_gradient = key_gradient[PROMPT_LENGTH:].reshape(RESPONSE_LENGTH, KEY_VALUE_HEADS * HEAD_WIDTH).astype(jnp.bfloat16)
        response_value_gradient = value_gradient[PROMPT_LENGTH:].reshape(RESPONSE_LENGTH, KEY_VALUE_HEADS * HEAD_WIDTH).astype(jnp.bfloat16)
        new_sums = (sums[0] + key_gradient[:PROMPT_LENGTH], sums[1] + value_gradient[:PROMPT_LENGTH])
        return new_sums, (grad_query, response_key_gradient, response_value_gradient)

    initial_sums = (jnp.zeros((PROMPT_LENGTH, KEY_VALUE_HEADS, HEAD_WIDTH), jnp.float32), jnp.zeros((PROMPT_LENGTH, KEY_VALUE_HEADS, HEAD_WIDTH), jnp.float32))
    (prompt_key_grads, prompt_value_grads), (grad_q, grad_k_resp, grad_v_resp) = lax.scan(
        one_response, initial_sums, (response_query, response_key, response_value, grad_out, lengths))
    prompt_key_gradient = prompt_key_grads.reshape(PROMPT_LENGTH, KEY_VALUE_HEADS * HEAD_WIDTH).astype(jnp.bfloat16)
    prompt_value_gradient = prompt_value_grads.reshape(PROMPT_LENGTH, KEY_VALUE_HEADS * HEAD_WIDTH).astype(jnp.bfloat16)
    return (grad_q, grad_k_resp, grad_v_resp, prompt_key_gradient, prompt_value_gradient)
```

```python
import functools

import jax
import jax.numpy as jnp
from jax import lax
from jax.experimental import pallas as pl
from jax.experimental.pallas import tpu as pltpu
from jax.sharding import PartitionSpec as P

HEADS = 7
D = 128
RESP = 4096
PROMPT = 2048
SCALE = D**-0.5
LOG2E = 1.4426950408889634
KC = 512
f32, bf16 = jnp.float32, jnp.bfloat16
MESH = pl.DeviceIdType.MESH
ANY = pl.BlockSpec(memory_space=pl.ANY)
VMEM = pl.BlockSpec(memory_space=pltpu.VMEM)
SMEM = pl.BlockSpec(memory_space=pltpu.SMEM)


def dot(a, b):
    return jnp.dot(a, b, preferred_element_type=f32)


def place():
    r, b = lax.axis_index("resp"), lax.axis_index("blk")
    z, y, c = b // 4, lax.rem(b // 2, 2), lax.rem(b, 2)
    return r, b, z, y, c


def aligned(start, size):
    return pl.ds(pl.multiple_of(start, size), size)


def mod8(value):
    return lax.rem(value + 16, 8)


def barrier(peers):
    sem = pltpu.get_barrier_semaphore()
    for peer in peers:
        pl.semaphore_signal(sem, inc=1, device_id=peer, device_id_type=MESH)
    pl.semaphore_wait(sem, len(peers))


def gather_kernel(
    q, g, rk, rv, pk, pv, qh, gh, kr, vr, kp, vp,
    own_sem, sib_s, sib_r, ky_s, ky_r, kz_s, kz_r, vz_s, vz_r, vy_s, vy_r,
):
    r, b, z, y, c = place()
    p = z * 2 + y
    sib = (r, b + 1 - 2 * c)
    yn = (r, b + 2 - 4 * y)
    zr = (r, lax.rem(b + 4, 32))
    zl = (r, lax.rem(b + 28, 32))
    barrier((sib, yn, zr, zl))

    def swap(i, src, dst, start, rows, width):
        mine = pltpu.make_async_copy(
            src.at[:, aligned(c * width, width)], dst.at[aligned(start, rows), :], own_sem.at[i]
        )
        theirs = pltpu.make_async_remote_copy(
            src_ref=src.at[:, aligned((1 - c) * width, width)],
            dst_ref=dst.at[aligned(start, rows), :],
            send_sem=sib_s.at[i],
            recv_sem=sib_r.at[i],
            device_id=sib,
            device_id_type=MESH,
        )
        mine.start()
        theirs.start()
        return mine, theirs

    first = p * 256 + c * 128
    swaps = [
        swap(0, pk, kp, p * 128 + c * 64, 64, 128),
        swap(1, pv, vp, p * 128 + c * 64, 64, 128),
        swap(2, rk, kr, first, 128, 128),
        swap(3, rv, vr, first, 128, 128),
        swap(4, q, qh, c * 128, 128, 896),
        swap(5, g, gh, c * 128, 128, 896),
    ]
    for mine, theirs in swaps[:4]:
        mine.wait()
        theirs.wait_recv()

    sent = []

    def send(ref, start, rows, to, s_sem, r_sem):
        copy = pltpu.make_async_remote_copy(
            src_ref=ref.at[aligned(start, rows), :],
            dst_ref=ref.at[aligned(start, rows), :],
            send_sem=s_sem,
            recv_sem=r_sem,
            device_id=to,
            device_id_type=MESH,
        )
        copy.start()
        sent.append(copy)
        return copy

    arrays = ((0, kp, vp, 128), (1, kr, vr, 256))
    pending_ky, pending_kz, pending_vz, pending_vy = [], [], [], []

    def start_ky():
        for i, kx, _, n in arrays:
            pending_ky.append(send(kx, p * n, n, yn, ky_s.at[i], ky_r.at[i]))

    def start_vz(step):
        for i, _, vx, n in arrays:
            for way, to in ((0, zr), (1, zl)):
                t = mod8(z - step + 1) if way == 0 else mod8(z + step - 1)
                start, rows = (t * 2 + y) * n, n
                if step == 4:
                    rows = n // 2
                    start = start + way * rows
                k = i * 8 + way * 4 + step - 1
                pending_vz.append(send(vx, start, rows, to, vz_s.at[k], vz_r.at[k]))

    def start_vy(slots):
        for i, _, vx, n in arrays:
            for slot, t in slots:
                k = i * 8 + slot
                pending_vy.append(send(vx, (t * 2 + y) * n, n, yn, vy_s.at[k], vy_r.at[k]))

    def start_kz(step):
        for i, kx, _, n in arrays:
            for way, to in ((0, zr), (1, zl)):
                t = mod8(z - step + 1) if way == 0 else mod8(z + step - 1)
                start, rows = t * 2 * n, 2 * n
                if step == 4:
                    rows = n
                    start = start + way * rows
                k = i * 8 + way * 4 + step - 1
                pending_kz.append(send(kx, start, rows, to, kz_s.at[k], kz_r.at[k]))

    def drain(pending):
        for copy in pending:
            copy.wait_recv()
        pending.clear()

    start_ky()
    start_vz(1)
    start_vy([(0, z)])
    drain(pending_ky)
    start_kz(1)
    for step in range(2, 5):
        drain(pending_vz)
        start_vz(step)
        start_vy([(step - 1, mod8(z - step + 1)), (step + 3, mod8(z + step - 1))])
        drain(pending_kz)
        start_kz(step)
    drain(pending_vz)
    start_vy([(4, mod8(z + 4))])
    drain(pending_kz)
    drain(pending_vy)
    for mine, theirs in swaps[4:]:
        mine.wait()
        theirs.wait_recv()
    for _, theirs in swaps:
        theirs.wait_send()
    for copy in sent:
        copy.wait_send()


def compute_kernel(
    length, q, g_in, kr, vr, kp, vp, dq, dkr, dvr, dkp, dvp,
    g, kt, qt, gt, pb, dpb, mb, dk, dv,
):
    _, _, z, y, c = place()
    chip = z * 2 + y
    for i in range(PROMPT // 512):
        kt[:, i * 512 : (i + 1) * 512] = kp[i * 512 : (i + 1) * 512, :].T

    @pl.loop(0, RESP // 512)
    def _(i):
        kt[:, aligned(PROMPT + i * 512, 512)] = kr[aligned(i * 512, 512), :].T

    row = lax.broadcasted_iota(jnp.int32, (256, 896), 0) + chip * 256
    g[...] = jnp.where(row < length[0], g_in[...].astype(f32), 0.0).astype(bf16)
    dk[...] = jnp.zeros_like(dk)
    dv[...] = jnp.zeros_like(dv)
    n_resp = chip // 2

    def head(j, _):
        cols = aligned(j * 128, 128)
        qj = q[:, cols]
        gj = g[:, cols]
        qt[...] = qj.T
        gt[...] = gj.T

        def stats(k_src, v_src, start, base, carry, masked):
            m, l, d = carry
            s = dot(k_src[aligned(start, KC), :], qt[...]) * (SCALE * LOG2E)
            dp = dot(v_src[aligned(start, KC), :], gt[...])
            if masked:
                key = lax.broadcasted_iota(jnp.int32, s.shape, 0) + start
                pos = lax.broadcasted_iota(jnp.int32, s.shape, 1) + chip * 256
                s = jnp.where(key <= pos, s, -jnp.inf)
            top = jnp.maximum(m, jnp.max(s, axis=0, keepdims=True))
            back = jnp.exp2(m - top)
            w = jnp.exp2(s - top)
            l = l * back + jnp.sum(w, axis=0, keepdims=True)
            d = d * back + jnp.sum(w * dp, axis=0, keepdims=True)
            pb[aligned(base, KC), :] = w.astype(bf16)
            dpb[aligned(base, KC), :] = dp
            mb[base // KC] = jnp.broadcast_to(top, (8, 256))
            return top, l, d

        carry = (
            jnp.full((1, 256), -jnp.inf, f32),
            jnp.zeros((1, 256), f32),
            jnp.zeros((1, 256), f32),
        )
        carry = lax.fori_loop(
            0, PROMPT // KC, lambda i, x: stats(kp, vp, i * KC, i * KC, x, False), carry, unroll=2
        )
        carry = lax.fori_loop(
            0, n_resp, lambda i, x: stats(kr, vr, i * KC, PROMPT + i * KC, x, False), carry
        )
        m, l, d = stats(kr, vr, n_resp * KC, PROMPT + n_resp * KC, carry, True)
        inv = 1.0 / l
        d = d * inv

        def grads(base, acc):
            r = jnp.exp2(mb[base // KC][0:1] - m) * inv
            w = pb[aligned(base, KC), :].astype(f32) * r
            ds = (w * (dpb[aligned(base, KC), :] - d)).astype(bf16)
            dk[aligned(base, KC), :] += dot(ds, qj)
            dv[aligned(base, KC), :] += dot(w.astype(bf16), gj)
            return acc + dot(kt[:, aligned(base, KC)], ds)

        acc = lax.fori_loop(
            0, PROMPT // KC, lambda i, x: grads(i * KC, x), jnp.zeros((128, 256), f32), unroll=2
        )
        acc = lax.fori_loop(0, n_resp + 1, lambda i, x: grads(PROMPT + i * KC, x), acc)
        dq[:, cols] = (acc.T * SCALE).astype(bf16)
        return 0

    lax.fori_loop(0, HEADS, head, 0)
    dkp[...] = (dk[:PROMPT, :] * SCALE).astype(bf16)
    dvp[...] = dv[:PROMPT, :].astype(bf16)
    dkr[...] = (dk[PROMPT:, :] * SCALE).astype(bf16)
    dvr[...] = dv[PROMPT:, :].astype(bf16)


def reduce_kernel(
    dq, dkr, dvr, dkp, dvp, gq, gk, gv, pkg, pvg,
    k_out, k_in, v_out, v_in, v_y, ky_out, ky_in, fin, x_in, xs, yz_in, g_out,
    q_sem, kz_s, kz_r, vz_s, vz_r, vy_s, vy_r, ky_s, ky_r, f_sem, x_s, x_r, yz_s, yz_r, g_s, g_r,
):
    r, b, z, y, c = place()
    x, y_hi = r // 2, lax.rem(r, 2)
    p = z * 2 + y
    sib = (r, b + 1 - 2 * c)
    yn = (r, b + 2 - 4 * y)
    zr = (r, lax.rem(b + 4, 32))
    zl = (r, lax.rem(b + 28, 32))

    def yz_peer(o):
        yh = lax.rem(y_hi + o // 16, 2)
        zz = lax.rem(z + lax.rem(o // 2, 8), 8)
        yl = lax.rem(y + lax.rem(o, 2), 2)
        return yh, zz, yl

    sem = pltpu.get_barrier_semaphore()

    @pl.loop(1, 32)
    def _(o):
        yh, zz, yl = yz_peer(o)
        pl.semaphore_signal(sem, inc=1, device_id=(x * 2 + yh, zz * 4 + yl * 2 + c), device_id_type=MESH)

    @pl.loop(1, 16)
    def _(o):
        rr = lax.rem(r + o // 2, 8)
        cc = lax.rem(c + lax.rem(o, 2), 2)
        pl.semaphore_signal(sem, inc=1, device_id=(rr, p * 2 + cc), device_id_type=MESH)

    pl.semaphore_wait(sem, 46)
    sent = []

    def send(src, dst, to, s_sem, r_sem):
        copy = pltpu.make_async_remote_copy(
            src_ref=src, dst_ref=dst, send_sem=s_sem, recv_sem=r_sem, device_id=to, device_id_type=MESH
        )
        copy.start()
        sent.append(copy)
        return copy

    vy = {}

    def start_vy(slot, t):
        vy[slot] = send(
            dvr.at[aligned((t * 2 + 1 - y) * 256, 256), :], v_y.at[slot], yn, vy_s.at[slot], vy_r.at[slot]
        )

    start_vy(4, mod8(z + 4))
    kz = {}
    t4 = mod8(z + 4)
    kz[0, 1] = send(dkr.at[aligned(t4 * 512, 256), :], k_in.at[0, 0, 0:256], zr, kz_s.at[0], kz_r.at[0])
    kz[1, 1] = send(
        dkr.at[aligned(t4 * 512 + 256, 256), :], k_in.at[1, 0, 256:512], zl, kz_s.at[4], kz_r.at[4]
    )
    xc = []
    for dx in range(1, 4):
        xx = lax.rem(x + dx, 4)
        for i, src in ((0, dkp), (1, dvp)):
            k = (dx - 1) * 2 + i
            xc.append(send(src.at[:, xx], x_in.at[dx - 1, i], (xx * 2 + y_hi, b), x_s.at[k], x_r.at[k]))
    for step in (3, 2, 1):
        start_vy(step, mod8(z + step))
        start_vy(8 - step, mod8(z - step))
    start_vy(0, z)
    mine_q = pltpu.make_async_copy(
        dq.at[aligned(c * 128, 128), :], gq.at[:, aligned(c * 896, 896)], q_sem.at[0]
    )
    mine_q.start()
    their_q = send(
        dq.at[aligned((1 - c) * 128, 128), :], gq.at[:, aligned(c * 896, 896)], sib, q_sem.at[1], q_sem.at[2]
    )

    def v_own(t, slot, lo, rows):
        own = dvr[aligned((t * 2 + y) * 256 + lo, rows), :].astype(f32)
        return own + v_y[slot, lo : lo + rows, :].astype(f32)

    vz = {}
    vy[4].wait_recv()
    for way, to in ((0, zr), (1, zl)):
        lo = way * 128
        v_out[way, 0, lo : lo + 128, :] = v_own(t4, 4, lo, 128).astype(bf16)
        vz[way, 1] = send(
            v_out.at[way, 0, lo : lo + 128], v_in.at[way, 0, lo : lo + 128], to,
            vz_s.at[way * 4], vz_r.at[way * 4],
        )
    for step in range(2, 5):
        for way, to in ((0, zr), (1, zl)):
            far = 5 - step
            t = mod8(z + far) if way == 0 else mod8(z - far)
            kz[way, step - 1].wait_recv()
            own = dkr[aligned(t * 512, 512), :]
            if step == 2:
                lo = way * 256
                other = 256 - lo
                k_out[way, 1, lo : lo + 256, :] = (
                    own[lo : lo + 256, :].astype(f32) + k_in[way, 0, lo : lo + 256, :].astype(f32)
                ).astype(bf16)
                k_out[way, 1, other : other + 256, :] = own[other : other + 256, :]
            else:
                k_out[way, step - 1] = (own.astype(f32) + k_in[way, step - 2].astype(f32)).astype(bf16)
            k = way * 4 + step - 1
            kz[way, step] = send(k_out.at[way, step - 1], k_in.at[way, step - 1], to, kz_s.at[k], kz_r.at[k])
        for way, to in ((0, zr), (1, zl)):
            far = 5 - step
            t = mod8(z + far) if way == 0 else mod8(z - far)
            slot = far if way == 0 else 8 - far
            vy[slot].wait_recv()
            vz[way, step - 1].wait_recv()
            if step == 2:
                lo = way * 128
                other = 128 - lo
                v_out[way, 1, lo : lo + 128, :] = (
                    v_own(t, slot, lo, 128) + v_in[way, 0, lo : lo + 128, :].astype(f32)
                ).astype(bf16)
                v_out[way, 1, other : other + 128, :] = v_own(t, slot, other, 128).astype(bf16)
            else:
                v_out[way, step - 1] = (v_own(t, slot, 0, 256) + v_in[way, step - 2].astype(f32)).astype(bf16)
            k = way * 4 + step - 1
            vz[way, step] = send(v_out.at[way, step - 1], v_in.at[way, step - 1], to, vz_s.at[k], vz_r.at[k])
        if step == 2:
            for copy in xc:
                copy.wait_recv()
            for i, src in ((0, dkp), (1, dvp)):
                xs[i] = (
                    src[:, x].astype(f32)
                    + x_in[0, i].astype(f32)
                    + x_in[1, i].astype(f32)
                    + x_in[2, i].astype(f32)
                ).astype(bf16)

            def yz_copy(o):
                yh, zz, yl = yz_peer(o)
                return pltpu.make_async_remote_copy(
                    src_ref=xs.at[:, zz * 2 + yl, aligned(yh * 16, 16), :],
                    dst_ref=yz_in.at[o],
                    send_sem=yz_s.at[o],
                    recv_sem=yz_r.at[o],
                    device_id=(x * 2 + yh, zz * 4 + yl * 2 + c),
                    device_id_type=MESH,
                )

            @pl.loop(1, 32)
            def _(o):
                yz_copy(o).start()

    yz_in[0] = xs[:, p, aligned(y_hi * 16, 16), :]

    @pl.loop(1, 32)
    def _(o):
        yz_copy(o).wait()

    g_out[...] = jnp.sum(yz_in[...].astype(f32), axis=0).astype(bf16)
    core = r // 4
    part = lax.rem(r, 4)

    def g_copy(o, i, out):
        rr = lax.rem(r + o, 8)
        return (
            g_out.at[i],
            out.at[aligned(part * 16, 16), aligned(c * 128, 128)],
            g_s.at[i * 8 + o],
            g_r.at[i * 8 + part * 2 + c],
            (rr, p * 2 + core),
        )

    for i, out in ((0, pkg), (1, pvg)):
        for o in range(8):
            src, dst, s_sem, r_sem, to = g_copy(o, i, out)
            if o == 0:

                @pl.when(core == c)
                def _():
                    pltpu.make_async_copy(src, dst, r_sem).start()

                @pl.when(core != c)
                def _():
                    pltpu.make_async_remote_copy(
                        src_ref=src, dst_ref=dst, send_sem=s_sem, recv_sem=r_sem, device_id=to, device_id_type=MESH
                    ).start()
            else:
                send(src, dst, to, s_sem, r_sem)

    for way in (0, 1):
        kz[way, 4].wait_recv()
    total = dkr[aligned(z * 512, 512), :].astype(f32) + k_in[0, 3].astype(f32) + k_in[1, 3].astype(f32)
    ky_out[...] = total.astype(bf16).reshape(2, 256, D)
    ky = send(ky_out.at[1 - y], ky_in, yn, ky_s, ky_r)
    vy[0].wait_recv()
    for way in (0, 1):
        vz[way, 4].wait_recv()
    fin[1] = (v_own(z, 0, 0, 256) + v_in[0, 3].astype(f32) + v_in[1, 3].astype(f32)).astype(bf16)
    ky.wait_recv()
    k_mine = (
        dkr[aligned((z * 2 + y) * 256, 256), :].astype(f32)
        + k_in[0, 3, aligned(y * 256, 256), :].astype(f32)
        + k_in[1, 3, aligned(y * 256, 256), :].astype(f32)
    )
    fin[0] = (k_mine + ky_in[...].astype(f32)).astype(bf16)
    last = []
    for i, out in ((0, gk), (1, gv)):
        mine = pltpu.make_async_copy(
            fin.at[i, aligned(c * 128, 128), :], out.at[:, aligned(c * 128, 128)], f_sem.at[i]
        )
        mine.start()
        theirs = send(
            fin.at[i, aligned((1 - c) * 128, 128), :], out.at[:, aligned(c * 128, 128)], sib,
            f_sem.at[2 + i], f_sem.at[4 + i],
        )
        last.append((mine, theirs))
    for mine, theirs in last:
        mine.wait()
        theirs.wait_recv()
    mine_q.wait()
    their_q.wait_recv()
    for i, out in ((0, pkg), (1, pvg)):
        for k in range(8):
            pltpu.make_async_copy(g_out.at[i], out.at[0:16, 0:128], g_r.at[i * 8 + k]).wait()

        @pl.when(core != c)
        def _():
            pltpu.make_async_copy(g_out.at[i], out.at[0:16, 0:128], g_s.at[i * 8]).wait()

    for copy in sent:
        copy.wait_send()


def shards(q, rk, rv, pk, pv, go, lengths):
    rows = q.shape[1]
    q, rk, rv, go = q[0], rk[0], rv[0], go[0]
    dma = pltpu.SemaphoreType.DMA

    def out(*shape):
        return jax.ShapeDtypeStruct(shape, bf16)

    qh, gh, kr, vr, kp, vp = pl.pallas_call(
        gather_kernel,
        out_shape=(
            out(2 * rows, 896), out(2 * rows, 896), out(RESP, D), out(RESP, D), out(PROMPT, D), out(PROMPT, D),
        ),
        in_specs=[ANY] * 6,
        out_specs=(ANY,) * 6,
        scratch_shapes=[
            dma((6,)), dma((6,)), dma((6,)), dma((2,)), dma((2,)),
            dma((16,)), dma((16,)), dma((16,)), dma((16,)), dma((16,)), dma((16,)),
        ],
        compiler_params=pltpu.CompilerParams(collective_id=0, has_side_effects=True),
        name="gather",
    )(q, go, rk, rv, pk, pv)

    n_keys = PROMPT + RESP
    dq, dkr, dvr, dkp, dvp = pl.pallas_call(
        compute_kernel,
        out_shape=(out(2 * rows, 896), out(RESP, D), out(RESP, D), out(PROMPT, D), out(PROMPT, D)),
        in_specs=[SMEM] + [VMEM] * 6,
        out_specs=(VMEM,) * 5,
        scratch_shapes=[
            pltpu.VMEM((256, 896), bf16),
            pltpu.VMEM((D, n_keys), bf16),
            pltpu.VMEM((D, 256), bf16),
            pltpu.VMEM((D, 256), bf16),
            pltpu.VMEM((n_keys, 256), bf16),
            pltpu.VMEM((n_keys, 256), f32),
            pltpu.VMEM((n_keys // KC, 8, 256), f32),
            pltpu.VMEM((n_keys, D), f32),
            pltpu.VMEM((n_keys, D), f32),
        ],
        compiler_params=pltpu.CompilerParams(vmem_limit_bytes=58 * 2**20),
        name="grads",
    )(lengths, qh, gh, kr, vr, kp, vp)

    v = pltpu.VMEM
    gq, gk, gv, pkg, pvg = pl.pallas_call(
        reduce_kernel,
        out_shape=(out(rows, 1792), out(rows, 256), out(rows, 256), out(64, 256), out(64, 256)),
        in_specs=[VMEM] * 5,
        out_specs=(VMEM,) * 5,
        scratch_shapes=[
            v((2, 4, 512, D), bf16), v((2, 4, 512, D), bf16), v((2, 4, 256, D), bf16), v((2, 4, 256, D), bf16),
            v((8, 256, D), bf16), v((2, 256, D), bf16), v((256, D), bf16), v((2, 256, D), bf16),
            v((3, 2, 16, 32, D), bf16), v((2, 16, 32, D), bf16), v((32, 2, 16, D), bf16), v((2, 16, D), bf16),
            dma((3,)), dma((8,)), dma((8,)), dma((8,)), dma((8,)), dma((8,)), dma((8,)), dma, dma,
            dma((6,)), dma((6,)), dma((6,)), dma((32,)), dma((32,)), dma((16,)), dma((16,)),
        ],
        compiler_params=pltpu.CompilerParams(
            collective_id=1, has_side_effects=True, vmem_limit_bytes=40 * 2**20
        ),
        name="reduce",
    )(dq, dkr, dvr, dkp.reshape(16, 4, 32, D), dvp.reshape(16, 4, 32, D))
    return gq[None], gk[None], gv[None], pkg, pvg


def solution(mesh):
    in_specs = (
        P("resp", "blk", None),
        P("resp", "blk", None),
        P("resp", "blk", None),
        P("blk", None),
        P("blk", None),
        P("resp", "blk", None),
        P("resp"),
    )
    out_specs = (
        P("resp", "blk", None),
        P("resp", "blk", None),
        P("resp", "blk", None),
        P("blk", None),
        P("blk", None),
    )
    return jax.shard_map(shards, mesh=mesh, in_specs=in_specs, out_specs=out_specs, check_vma=False)
```

```python
import functools

import jax
import jax.numpy as jnp
from jax import lax
from jax.experimental import pallas as pl
from jax.experimental.pallas import tpu as pltpu
from jax.sharding import PartitionSpec as P

HEADS = 7
D = 128
RESP = 4096
PROMPT = 2048
SCALE = D**-0.5
LOG2E = 1.4426950408889634
KC = 512
f32, bf16 = jnp.float32, jnp.bfloat16
MESH = pl.DeviceIdType.MESH
ANY = pl.BlockSpec(memory_space=pl.ANY)
VMEM = pl.BlockSpec(memory_space=pltpu.VMEM)
SMEM = pl.BlockSpec(memory_space=pltpu.SMEM)


def dot(a, b):
    return jnp.dot(a, b, preferred_element_type=f32)


def place():
    r, b = lax.axis_index("resp"), lax.axis_index("blk")
    z, y, c = b // 4, lax.rem(b // 2, 2), lax.rem(b, 2)
    return r, b, z, y, c


def aligned(start, size):
    return pl.ds(pl.multiple_of(start, size), size)


def mod8(value):
    return lax.rem(value + 16, 8)


class Remote:
    def __init__(self, parts):
        self.parts = parts

    def make(self):
        src, dst, to, s_sem, r_sem = self.parts()
        return pltpu.make_async_remote_copy(
            src_ref=src, dst_ref=dst, send_sem=s_sem, recv_sem=r_sem, device_id=to, device_id_type=MESH
        )

    def start(self):
        self.make().start()

    def wait_recv(self):
        self.make().wait_recv()

    def wait_send(self):
        self.make().wait_send()


def fused_kernel(
    length, q, g, rk, rv, pk, pv, gq, gk, gv, pkg, pvg,
    qh, gh, qt, gt, ks, vs, pb, db, mb, ms, ls, ds, cen, sb, sd, dqt, dqs,
    dkr, dvr, dkp, dvp, k_in, v_in, v_y, ky_out, ky_in, fin, x_in, xs, yz_in, g_out,
    own_sem, sib_s, sib_r, qg_own, qg_s, qg_r,
    ky_s, ky_r, kz_s, kz_r, vz_s, vz_r, vy_s, vy_r,
    rkz_s, rkz_r, rvz_s, rvz_r, rvy_s, rvy_r, rky_s, rky_r, f_sem,
    x_s, x_r, yz_s, yz_r, g_s, g_r, dq_own, dq_s, dq_r,
):
    r, b, z, y, c = place()
    x, y_hi = r // 2, lax.rem(r, 2)
    p = z * 2 + y
    sib = (r, b + 1 - 2 * c)
    yn = (r, b + 2 - 4 * y)
    zr = (r, lax.rem(b + 4, 32))
    zl = (r, lax.rem(b + 28, 32))
    ways = ((0, zr), (1, zl))

    def yz_peer(o):
        yh = lax.rem(y_hi + o // 16, 2)
        zz = lax.rem(z + lax.rem(o // 2, 8), 8)
        yl = lax.rem(y + lax.rem(o, 2), 2)
        return yh, zz, yl

    sem = pltpu.get_barrier_semaphore()

    @pl.loop(1, 32)
    def _(o):
        yh, zz, yl = yz_peer(o)
        pl.semaphore_signal(sem, inc=1, device_id=(x * 2 + yh, zz * 4 + yl * 2 + c), device_id_type=MESH)

    @pl.loop(1, 16)
    def _(o):
        rr = lax.rem(r + o // 2, 8)
        cc = lax.rem(c + lax.rem(o, 2), 2)
        pl.semaphore_signal(sem, inc=1, device_id=(rr, p * 2 + cc), device_id_type=MESH)

    pl.semaphore_wait(sem, 46)
    sent = {}

    def send(key, parts):
        copy = Remote(parts)
        copy.start()
        sent[key] = copy
        return copy

    def drain(pending):
        for copy in pending:
            copy.wait_recv()

    def swap(src, dst, width, mine_sem, s_sem, r_sem, h=0):
        w = width * D
        mine = pltpu.make_async_copy(src.at[:, aligned(c * w + h * D, D)], dst, mine_sem)
        mine.start()
        theirs = send(
            ("swap", len(sent)), lambda: (src.at[:, aligned((1 - c) * w + h * D, D)], dst, sib, s_sem, r_sem)
        )
        return mine, theirs

    first = PROMPT + p * 256 + c * 128
    swaps = []
    for i, (src, dst) in enumerate(
        (
            (pk, ks.at[aligned(p * 128 + c * 64, 64), :]),
            (pv, vs.at[aligned(p * 128 + c * 64, 64), :]),
            (rk, ks.at[aligned(first, 128), :]),
            (rv, vs.at[aligned(first, 128), :]),
        )
    ):
        swaps.append(swap(src, dst, 1, own_sem.at[i], sib_s.at[i], sib_r.at[i]))
    qg_swaps = []
    for i, (src, dst) in enumerate(((q, qh), (g, gh))):
        for h in range(HEADS):
            k = i * HEADS + h
            to = dst.at[h, aligned(c * 128, 128), :]
            qg_swaps.append(swap(src, to, HEADS, qg_own.at[k], qg_s.at[k], qg_r.at[k], h))
    for mine, theirs in swaps:
        mine.wait()
        theirs.wait_recv()

    def push(key, ref, span, to, s_sems, r_sems, k):
        def parts():
            part = ref.at[aligned(*span()), :]
            return part, part, to, s_sems.at[k], r_sems.at[k]

        return send(key, parts)

    base_of, rows_of = (0, PROMPT), (128, 256)
    pend = {}

    def start_ky(i):
        n = rows_of[i]
        pend["ky", i] = [
            push(("ky", i), ks, lambda: (base_of[i] + p * n, n), yn, ky_s, ky_r, i)
        ]

    def start_vz(i, step):
        n = rows_of[i]
        out = []
        for way, to in ways:

            def span(way=way):
                t = mod8(z - step + 1) if way == 0 else mod8(z + step - 1)
                start = base_of[i] + (t * 2 + y) * n
                return (start + way * (n // 2), n // 2) if step == 4 else (start, n)

            k = i * 8 + way * 4 + step - 1
            out.append(push(("vz", k), vs, span, to, vz_s, vz_r, k))
        pend["vz", i, step] = out

    def start_vy(i, slot):
        n = rows_of[i]
        k = i * 8 + slot

        def span():
            return base_of[i] + (mod8(z - slot) * 2 + y) * n, n

        pend["vy", i, slot] = [push(("vy", k), vs, span, yn, vy_s, vy_r, k)]

    def start_kz(i, step):
        n = rows_of[i]
        out = []
        for way, to in ways:

            def span(way=way):
                t = mod8(z - step + 1) if way == 0 else mod8(z + step - 1)
                start = base_of[i] + t * 2 * n
                return (start + way * n, n) if step == 4 else (start, 2 * n)

            k = i * 8 + way * 4 + step - 1
            out.append(push(("kz", k), ks, span, to, kz_s, kz_r, k))
        pend["kz", i, step] = out

    def ring(i, step):
        drain(pend["vz", i, step - 1])
        if step < 5:
            start_vz(i, step)
            start_vy(i, step - 1)
            start_vy(i, 9 - step)
        else:
            start_vy(i, 4)
        drain(pend["kz", i, step - 1])
        if step < 5:
            start_kz(i, step)

    start_ky(0)
    start_vz(0, 1)
    start_vy(0, 0)
    start_ky(1)
    start_vy(1, 0)
    drain(pend["ky", 0])
    start_kz(0, 1)

    dkr[...] = jnp.zeros_like(dkr)
    dvr[...] = jnp.zeros_like(dvr)
    dqt[...] = jnp.zeros_like(dqt)
    ms[...] = jnp.full_like(ms, -1e30)
    ls[...] = jnp.zeros_like(ls)
    ds[...] = jnp.zeros_like(ds)
    for mine, theirs in qg_swaps:
        mine.wait()
        theirs.wait_recv()
    live = lax.broadcasted_iota(jnp.int32, (256, D), 0) + p * 256 < length[0]
    for h in range(HEADS):
        gh[h] = jnp.where(live, gh[h].astype(f32), 0.0).astype(bf16)
        qt[h] = qh[h].T
        gt[h] = gh[h].T
    drain(pend["ky", 1])
    drain(pend["vy", 1, 0])
    own_rows = aligned(PROMPT + z * KC, KC)
    middle = jnp.mean(vs[own_rows, :].astype(f32), axis=0, keepdims=True)
    middle = jnp.broadcast_to(middle, (16, D)).astype(bf16)
    for h in range(HEADS):
        cen[h] = dot(middle, gt[h])[0:1]

    def stats(i, masked):
        rows = aligned(i * KC, KC)
        kc = ks[rows, :]
        vc = vs[rows, :]

        def logits(h):
            s = dot(kc, qt[h])
            if masked:
                key = lax.broadcasted_iota(jnp.int32, s.shape, 0)
                pos = lax.broadcasted_iota(jnp.int32, s.shape, 1) + y * 256
                s = jnp.where(key <= pos, s, -jnp.inf)
            sb[h % 2] = s
            return jnp.maximum(ms[h], jnp.max(s, axis=0, keepdims=True) * (SCALE * LOG2E))

        top = logits(0)
        for h in range(HEADS):
            ahead = logits(h + 1) if h + 1 < HEADS else None
            dp = dot(vc, gt[h]) - cen[h]
            back = jnp.exp2(ms[h] - top)
            w = jnp.exp2(sb[h % 2] * (SCALE * LOG2E) - top)
            ls[h] = ls[h] * back + jnp.sum(w, axis=0, keepdims=True)
            ds[h] = ds[h] * back + jnp.sum(w * dp, axis=0, keepdims=True)
            pb[h, rows, :] = w.astype(bf16)
            db[h, rows, :] = dp.astype(bf16)
            mb[i, h] = top
            ms[h] = top
            top = ahead

    stats(4 + z, True)
    ring(0, 2)
    ring(0, 3)
    start_vz(1, 1)
    start_kz(1, 1)
    ring(0, 4)
    ring(0, 5)
    for slot in range(8):
        drain(pend["vy", 0, slot])

    def vy_ready(*slots):
        for slot in slots:
            drain(pend["vy", 1, slot])

    stats_events = {
        2: (lambda: ring(1, 2),),
        4: (lambda: ring(1, 3), lambda: vy_ready(1, 7)),
        6: (lambda: ring(1, 4), lambda: vy_ready(2, 6)),
        8: (lambda: ring(1, 5), lambda: vy_ready(3, 5)),
        10: (lambda: vy_ready(4),),
    }

    def play(events, n):
        for k, acts in events.items():

            @pl.when(n == k)
            def _():
                for act in acts:
                    act()

    @pl.loop(0, 11)
    def _(n):
        play(stats_events, n)
        j = n - 4
        delta = jnp.where(lax.rem(n, 2) == 0, j // 2 + 1, 7 - j // 2)
        t = z - delta

        @pl.when((n < 4) | (t >= 0))
        def _():
            stats(jnp.where(n < 4, n, 4 + t), False)

    for h in range(HEADS):
        inv = 1.0 / ls[h]
        ls[h] = inv
        ds[h] = ds[h] * inv

    def grads(i):
        rows = aligned(i * KC, KC)
        kt = ks[rows, :].T
        dk = jnp.zeros((KC, D), f32)
        dv = jnp.zeros((KC, D), f32)
        for h in range(HEADS):
            w = pb[h, rows, :].astype(f32) * (jnp.exp2(mb[i, h] - ms[h]) * ls[h])
            d_logit = (w * (db[h, rows, :].astype(f32) - ds[h])).astype(bf16)
            sd[h] = d_logit
            dk = dk + dot(d_logit, qh[h])
            dv = dv + dot(w.astype(bf16), gh[h])
        for h in range(HEADS):
            dqt[h] += dot(kt, sd[h])
        return (dk * SCALE).astype(bf16), dv.astype(bf16)

    kz, vz, vy = {}, {}, {}
    xc = []

    def target(way, far):
        return mod8(z + far) if way == 0 else mod8(z - far)

    def send_vy(slot):
        def parts():
            return dvr.at[mod8(z + slot), 1 - y], v_y.at[slot], yn, rvy_s.at[slot], rvy_r.at[slot]

        vy[slot] = send(("rvy", slot), parts)

    def x_send():
        for dx in range(1, 4):
            for i, src in ((0, dkp), (1, dvp)):

                def parts(dx=dx, i=i, src=src):
                    k = (dx - 1) * 2 + i
                    xx = lax.rem(x + dx, 4)
                    return src.at[:, xx], x_in.at[dx - 1, i], (xx * 2 + y_hi, b), x_s.at[k], x_r.at[k]

                xc.append(send(("x", dx, i), parts))

    def add(ref, index, *terms):
        total = ref[index].astype(f32)
        for term in terms:
            total = total + term.astype(f32)
        ref[index] = total.astype(bf16)

    def k_step(step):
        for way, to in ways:
            t = target(way, 5 - step)
            half = pl.ds(way * 256, 256)

            def parts(way=way, to=to, half=half):
                t = target(way, 5 - step)
                k = way * 4 + step - 1
                src, dst = dkr.at[t], k_in.at[way, step - 1]
                if step == 1:
                    src, dst = dkr.at[t, half], k_in.at[way, 0, half]
                return src, dst, to, rkz_s.at[k], rkz_r.at[k]

            if step == 1:
                kz[way, 1] = send(("rkz", way, 1), parts)
                continue
            kz[way, step - 1].wait_recv()
            if step == 2:
                add(dkr, (t, half), k_in[way, 0, half])
            else:
                add(dkr, (t,), k_in[way, step - 2])
            kz[way, step] = send(("rkz", way, step), parts)

    def v_step(step):
        far = 5 - step
        if step == 1:
            vy[4].wait_recv()
            add(dvr, (mod8(z + 4), y), v_y[4])
        for way, to in ways:
            t = target(way, far)
            half = pl.ds(way * 128, 128)

            def parts(way=way, to=to, half=half):
                t = target(way, far)
                k = way * 4 + step - 1
                src, dst = dvr.at[t, y], v_in.at[way, step - 1]
                if step == 1:
                    src, dst = dvr.at[t, y, half], v_in.at[way, 0, half]
                return src, dst, to, rvz_s.at[k], rvz_r.at[k]

            if step == 1:
                vz[way, 1] = send(("rvz", way, 1), parts)
                continue
            slot = far if way == 0 else 8 - far
            vy[slot].wait_recv()
            vz[way, step - 1].wait_recv()
            if step == 2:
                add(dvr, (t, y), v_y[slot])
                add(dvr, (t, y, half), v_in[way, 0, half])
            else:
                add(dvr, (t, y), v_y[slot], v_in[way, step - 2])
            vz[way, step] = send(("rvz", way, step), parts)

    def yz_copy(o):
        yh, zz, yl = yz_peer(o)
        return pltpu.make_async_remote_copy(
            src_ref=xs.at[:, zz * 2 + yl, aligned(yh * 16, 16), :],
            dst_ref=yz_in.at[o],
            send_sem=yz_s.at[o],
            recv_sem=yz_r.at[o],
            device_id=(x * 2 + yh, zz * 4 + yl * 2 + c),
            device_id_type=MESH,
        )

    def yz_send():
        for copy in xc:
            copy.wait_recv()
        for i, src in ((0, dkp), (1, dvp)):
            xs[i] = (
                src[:, x].astype(f32) + x_in[0, i].astype(f32) + x_in[1, i].astype(f32) + x_in[2, i].astype(f32)
            ).astype(bf16)

        @pl.loop(1, 32)
        def _(o):
            yz_copy(o).start()

    def both(far):
        send_vy(far)
        send_vy(8 - far)

    grads_events = {
        4: (x_send,),
        5: (lambda: k_step(1), lambda: send_vy(4)),
        7: (lambda: both(3), lambda: k_step(2), lambda: v_step(1)),
        9: (lambda: both(2), lambda: k_step(3), lambda: v_step(2)),
        11: (lambda: both(1), lambda: k_step(4), lambda: v_step(3), yz_send),
    }

    @pl.loop(0, 12)
    def _(n):
        play(grads_events, n)
        j = n - 4
        far = 4 - (j + 1) // 2
        t = mod8(jnp.where(lax.rem(j + 8, 2) == 1, z + far, z - far))

        @pl.when((n < 4) | (t <= z))
        def _():
            dk, dv = grads(jnp.where(n < 4, n, 4 + t))

            @pl.when(n < 4)
            def _():
                dkp[pl.ds(n * 4, 4)] = dk.reshape(4, 4, 32, D)
                dvp[pl.ds(n * 4, 4)] = dv.reshape(4, 4, 32, D)

            @pl.when(n >= 4)
            def _():
                dkr[t] = dk
                dvr[t] = dv.reshape(2, 256, D)

    send_vy(0)
    v_step(4)

    dq_copies = []
    for h in range(HEADS):
        dqs[h] = (dqt[h].T * SCALE).astype(bf16)
        to = gq.at[:, aligned(c * 896 + h * D, D)]
        mine = pltpu.make_async_copy(dqs.at[h, aligned(c * 128, 128), :], to, dq_own.at[h])
        mine.start()
        theirs = send(
            ("dq", h),
            lambda h=h, to=to: (dqs.at[h, aligned((1 - c) * 128, 128), :], to, sib, dq_s.at[h], dq_r.at[h]),
        )
        dq_copies.append((mine, theirs))

    for way in (0, 1):
        kz[way, 4].wait_recv()
    total = dkr[z].astype(f32) + k_in[0, 3].astype(f32) + k_in[1, 3].astype(f32)
    ky_out[...] = total.astype(bf16).reshape(2, 256, D)
    ky = send(("rky",), lambda: (ky_out.at[1 - y], ky_in, yn, rky_s, rky_r))

    yz_in[0] = xs[:, p, aligned(y_hi * 16, 16), :]

    @pl.loop(1, 32)
    def _(o):
        yz_copy(o).wait()

    g_out[...] = jnp.sum(yz_in[...].astype(f32), axis=0).astype(bf16)
    core = r // 4
    part = lax.rem(r, 4)
    for i, out in ((0, pkg), (1, pvg)):
        for o in range(8):
            src = g_out.at[i]
            dst = out.at[aligned(part * 16, 16), aligned(c * 128, 128)]
            s_sem, r_sem = g_s.at[i * 8 + o], g_r.at[i * 8 + part * 2 + c]
            to = (lax.rem(r + o, 8), p * 2 + core)
            if o == 0:

                @pl.when(core == c)
                def _():
                    pltpu.make_async_copy(src, dst, r_sem).start()

                @pl.when(core != c)
                def _():
                    pltpu.make_async_remote_copy(
                        src_ref=src, dst_ref=dst, send_sem=s_sem, recv_sem=r_sem, device_id=to, device_id_type=MESH
                    ).start()
            else:
                send(("g", i, o), lambda a=(src, dst, to, s_sem, r_sem): a)

    vy[0].wait_recv()
    for way in (0, 1):
        vz[way, 4].wait_recv()
    fin[1] = (
        dvr[z, y].astype(f32) + v_y[0].astype(f32) + v_in[0, 3].astype(f32) + v_in[1, 3].astype(f32)
    ).astype(bf16)
    lines = aligned(y * 256, 256)
    ky.wait_recv()
    fin[0] = (
        dkr[z, lines].astype(f32) + k_in[0, 3, lines].astype(f32) + k_in[1, 3, lines].astype(f32)
        + ky_in[...].astype(f32)
    ).astype(bf16)
    last = []
    for i, out in ((0, gk), (1, gv)):
        to = out.at[:, aligned(c * 128, 128)]
        mine = pltpu.make_async_copy(fin.at[i, aligned(c * 128, 128), :], to, f_sem.at[i])
        mine.start()
        theirs = send(
            ("fin", i),
            lambda i=i, to=to: (fin.at[i, aligned((1 - c) * 128, 128), :], to, sib, f_sem.at[2 + i], f_sem.at[4 + i]),
        )
        last.append((mine, theirs))
    for mine, theirs in last + dq_copies:
        mine.wait()
        theirs.wait_recv()
    for i, out in ((0, pkg), (1, pvg)):
        for k in range(8):
            pltpu.make_async_copy(g_out.at[i], out.at[0:16, 0:128], g_r.at[i * 8 + k]).wait()

        @pl.when(core != c)
        def _():
            pltpu.make_async_copy(g_out.at[i], out.at[0:16, 0:128], g_s.at[i * 8]).wait()

    for copy in sent.values():
        copy.wait_send()


def shards(q, rk, rv, pk, pv, go, lengths):
    rows = q.shape[1]
    dma = pltpu.SemaphoreType.DMA
    n_keys = PROMPT + RESP

    def out(*shape):
        return jax.ShapeDtypeStruct(shape, bf16)

    def v(*shape, dtype=bf16):
        return pltpu.VMEM(shape, dtype)

    def w(*shape):
        return pltpu.VMEM(shape, f32)

    gq, gk, gv, pkg, pvg = pl.pallas_call(
        fused_kernel,
        out_shape=(out(rows, 1792), out(rows, 256), out(rows, 256), out(64, 256), out(64, 256)),
        in_specs=[SMEM] + [ANY] * 6,
        out_specs=(VMEM,) * 5,
        scratch_shapes=[
            v(HEADS, 256, D), v(HEADS, 256, D), v(HEADS, D, 256), v(HEADS, D, 256), v(n_keys, D), v(n_keys, D),
            v(HEADS, n_keys, 256), v(HEADS, n_keys, 256), w(n_keys // KC, HEADS, 1, 256),
            w(HEADS, 1, 256), w(HEADS, 1, 256), w(HEADS, 1, 256), w(HEADS, 1, 256),
            w(2, KC, 256), v(HEADS, KC, 256), w(HEADS, D, 256), v(HEADS, 256, D),
            v(8, 512, D), v(8, 2, 256, D), v(16, 4, 32, D), v(16, 4, 32, D),
            v(2, 4, 512, D), v(2, 4, 256, D), v(8, 256, D), v(2, 256, D), v(256, D), v(2, 256, D),
            v(3, 2, 16, 32, D), v(2, 16, 32, D), v(32, 2, 16, D), v(2, 16, D),
            dma((4,)), dma((4,)), dma((4,)), dma((14,)), dma((14,)), dma((14,)),
            dma((2,)), dma((2,)), dma((16,)), dma((16,)), dma((16,)), dma((16,)), dma((16,)), dma((16,)),
            dma((8,)), dma((8,)), dma((8,)), dma((8,)), dma((8,)), dma((8,)), dma, dma, dma((6,)),
            dma((6,)), dma((6,)), dma((32,)), dma((32,)), dma((16,)), dma((16,)), dma((7,)), dma((7,)), dma((7,)),
        ],
        compiler_params=pltpu.CompilerParams(
            collective_id=0, has_side_effects=True, vmem_limit_bytes=63 * 2**20
        ),
        name="fused",
    )(lengths, q[0], go[0], rk[0], rv[0], pk, pv)
    return gq[None], gk[None], gv[None], pkg, pvg


def solution(mesh):
    in_specs = (
        P("resp", "blk", None),
        P("resp", "blk", None),
        P("resp", "blk", None),
        P("blk", None),
        P("blk", None),
        P("resp", "blk", None),
        P("resp"),
    )
    out_specs = (
        P("resp", "blk", None),
        P("resp", "blk", None),
        P("resp", "blk", None),
        P("blk", None),
        P("blk", None),
    )
    return jax.shard_map(shards, mesh=mesh, in_specs=in_specs, out_specs=out_specs, check_vma=False)
```

```python
import functools

import jax
import jax.numpy as jnp
from jax import lax
from jax.experimental import pallas as pl
from jax.experimental.pallas import tpu as pltpu
from jax.sharding import PartitionSpec as P

HEADS = 7
D = 128
RESP = 4096
PROMPT = 2048
SCALE = D**-0.5
LOG2E = 1.4426950408889634
KC = 512
f32, bf16 = jnp.float32, jnp.bfloat16
MESH = pl.DeviceIdType.MESH
ANY = pl.BlockSpec(memory_space=pl.ANY)
VMEM = pl.BlockSpec(memory_space=pltpu.VMEM)
SMEM = pl.BlockSpec(memory_space=pltpu.SMEM)


def dot(a, b):
    return jnp.dot(a, b, preferred_element_type=f32)


def place():
    r, b = lax.axis_index("resp"), lax.axis_index("blk")
    z, y, c = b // 4, lax.rem(b // 2, 2), lax.rem(b, 2)
    return r, b, z, y, c


def aligned(start, size):
    return pl.ds(pl.multiple_of(start, size), size)


def mod8(value):
    return lax.rem(value + 16, 8)


class Remote:
    def __init__(self, parts):
        self.parts = parts

    def make(self):
        src, dst, to, s_sem, r_sem = self.parts()
        return pltpu.make_async_remote_copy(
            src_ref=src, dst_ref=dst, send_sem=s_sem, recv_sem=r_sem, device_id=to, device_id_type=MESH
        )

    def start(self):
        self.make().start()

    def wait_recv(self):
        self.make().wait_recv()

    def wait_send(self):
        self.make().wait_send()


def fused_kernel(
    length, q, g, rk, rv, pk, pv, gq, gk, gv, pkg, pvg,
    qh, gh, qt, gt, ks, vs, pb, db, mb, ms, ls, ds, cen, sb, sd, dqt, dqs,
    dkr, dvr, dkp, dvp, k_in, v_in, v_y, ky_out, ky_in, fin, x_in, xs, yz_in, g_out,
    own_sem, sib_s, sib_r, qg_own, qg_s, qg_r,
    ky_s, ky_r, kz_s, kz_r, vz_s, vz_r, vy_s, vy_r,
    rkz_s, rkz_r, rvz_s, rvz_r, rvy_s, rvy_r, rky_s, rky_r, f_sem,
    x_s, x_r, yz_s, yz_r, g_s, g_r, dq_own, dq_s, dq_r,
):
    r, b, z, y, c = place()
    x, y_hi = r // 2, lax.rem(r, 2)
    p = z * 2 + y
    sib = (r, b + 1 - 2 * c)
    yn = (r, b + 2 - 4 * y)
    zr = (r, lax.rem(b + 4, 32))
    zl = (r, lax.rem(b + 28, 32))
    ways = ((0, zr), (1, zl))

    def yz_peer(o):
        yh = lax.rem(y_hi + o // 16, 2)
        zz = lax.rem(z + lax.rem(o // 2, 8), 8)
        yl = lax.rem(y + lax.rem(o, 2), 2)
        return yh, zz, yl

    sem = pltpu.get_barrier_semaphore()

    @pl.loop(1, 32)
    def _(o):
        yh, zz, yl = yz_peer(o)
        pl.semaphore_signal(sem, inc=1, device_id=(x * 2 + yh, zz * 4 + yl * 2 + c), device_id_type=MESH)

    @pl.loop(1, 16)
    def _(o):
        rr = lax.rem(r + o // 2, 8)
        cc = lax.rem(c + lax.rem(o, 2), 2)
        pl.semaphore_signal(sem, inc=1, device_id=(rr, p * 2 + cc), device_id_type=MESH)

    first = PROMPT + p * 256 + c * 128
    kv_parts = (
        (pk, ks, p * 128 + c * 64, 64),
        (pv, vs, p * 128 + c * 64, 64),
        (rk, ks, first, 128),
        (rv, vs, first, 128),
    )
    qg_parts = [(i, h) for i in range(2) for h in range(HEADS)]
    own = []
    for i, (src, dst, start, rows) in enumerate(kv_parts):
        own.append(
            pltpu.make_async_copy(src.at[:, aligned(c * D, D)], dst.at[aligned(start, rows), :], own_sem.at[i])
        )
    for i, h in qg_parts:
        src, dst = ((q, qh), (g, gh))[i]
        own.append(
            pltpu.make_async_copy(
                src.at[:, aligned(c * 896 + h * D, D)],
                dst.at[h, aligned(c * 128, 128), :],
                qg_own.at[i * HEADS + h],
            )
        )
    for copy in own:
        copy.start()
    dkr[...] = jnp.zeros_like(dkr)
    dvr[...] = jnp.zeros_like(dvr)
    dqt[...] = jnp.zeros_like(dqt)
    ms[...] = jnp.full_like(ms, -1e30)
    ls[...] = jnp.zeros_like(ls)
    ds[...] = jnp.zeros_like(ds)
    for copy in own:
        copy.wait()

    def half_ready(half):
        rows = aligned(half * 128, 128)
        keep = lax.broadcasted_iota(jnp.int32, (128, D), 0) + (p * 256 + half * 128) < length[0]
        for h in range(HEADS):
            part = jnp.where(keep, gh[h, rows, :].astype(f32), 0.0).astype(bf16)
            gh[h, rows, :] = part
            gt[h, :, rows] = part.T
            qt[h, :, rows] = qh[h, rows, :].T

    half_ready(c)
    pl.semaphore_wait(sem, 46)
    sent = {}

    def send(key, parts):
        copy = Remote(parts)
        copy.start()
        sent[key] = copy
        return copy

    def drain(pending):
        for copy in pending:
            copy.wait_recv()

    swaps, qg_swaps = [], []
    for i, (src, dst, start, rows) in enumerate(kv_parts):

        def parts(i=i, src=src, dst=dst, start=start, rows=rows):
            return src.at[:, aligned((1 - c) * D, D)], dst.at[aligned(start, rows), :], sib, sib_s.at[i], sib_r.at[i]

        swaps.append(send(("kv", i), parts))
    for i, h in qg_parts:

        def parts(i=i, h=h):
            src, dst = ((q, qh), (g, gh))[i]
            k = i * HEADS + h
            col = aligned((1 - c) * 896 + h * D, D)
            return src.at[:, col], dst.at[h, aligned(c * 128, 128), :], sib, qg_s.at[k], qg_r.at[k]

        qg_swaps.append(send(("qg", i, h), parts))
    for copy in swaps:
        copy.wait_recv()

    def push(key, ref, span, to, s_sems, r_sems, k):
        def parts():
            part = ref.at[aligned(*span()), :]
            return part, part, to, s_sems.at[k], r_sems.at[k]

        return send(key, parts)

    base_of, rows_of = (0, PROMPT), (128, 256)
    pend = {}

    def start_ky(i):
        n = rows_of[i]
        pend["ky", i] = [
            push(("ky", i), ks, lambda: (base_of[i] + p * n, n), yn, ky_s, ky_r, i)
        ]

    def start_vz(i, step):
        n = rows_of[i]
        out = []
        for way, to in ways:

            def span(way=way):
                t = mod8(z - step + 1) if way == 0 else mod8(z + step - 1)
                start = base_of[i] + (t * 2 + y) * n
                return (start + way * (n // 2), n // 2) if step == 4 else (start, n)

            k = i * 8 + way * 4 + step - 1
            out.append(push(("vz", k), vs, span, to, vz_s, vz_r, k))
        pend["vz", i, step] = out

    def start_vy(i, slot):
        n = rows_of[i]
        k = i * 8 + slot

        def span():
            return base_of[i] + (mod8(z - slot) * 2 + y) * n, n

        pend["vy", i, slot] = [push(("vy", k), vs, span, yn, vy_s, vy_r, k)]

    def start_kz(i, step):
        n = rows_of[i]
        out = []
        for way, to in ways:

            def span(way=way):
                t = mod8(z - step + 1) if way == 0 else mod8(z + step - 1)
                start = base_of[i] + t * 2 * n
                return (start + way * n, n) if step == 4 else (start, 2 * n)

            k = i * 8 + way * 4 + step - 1
            out.append(push(("kz", k), ks, span, to, kz_s, kz_r, k))
        pend["kz", i, step] = out

    def ring(i, step):
        drain(pend["vz", i, step - 1])
        if step < 5:
            start_vz(i, step)
            start_vy(i, step - 1)
            start_vy(i, 9 - step)
        else:
            start_vy(i, 4)
        drain(pend["kz", i, step - 1])
        if step < 5:
            start_kz(i, step)

    for i in (0, 1):
        start_ky(i)
        start_vz(i, 1)
        start_vy(i, 0)
    for i in (0, 1):
        drain(pend["ky", i])
        start_kz(i, 1)
    for copy in qg_swaps:
        copy.wait_recv()
    half_ready(1 - c)
    drain(pend["vy", 1, 0])
    own_rows = aligned(PROMPT + z * KC, KC)
    middle = jnp.mean(vs[own_rows, :].astype(f32), axis=0, keepdims=True)
    middle = jnp.broadcast_to(middle, (16, D)).astype(bf16)
    for h in range(HEADS):
        cen[h] = dot(middle, gt[h])[0:1]

    def stats(i, masked):
        rows = aligned(i * KC, KC)
        kc = ks[rows, :]
        vc = vs[rows, :]

        def logits(h):
            s = dot(kc, qt[h])
            if masked:
                key = lax.broadcasted_iota(jnp.int32, s.shape, 0)
                pos = lax.broadcasted_iota(jnp.int32, s.shape, 1) + y * 256
                s = jnp.where(key <= pos, s, -jnp.inf)
            sb[h % 2] = s
            return jnp.maximum(ms[h], jnp.max(s, axis=0, keepdims=True) * (SCALE * LOG2E))

        top = logits(0)
        for h in range(HEADS):
            ahead = logits(h + 1) if h + 1 < HEADS else None
            dp = dot(vc, gt[h]) - cen[h]
            back = jnp.exp2(ms[h] - top)
            w = jnp.exp2(sb[h % 2] * (SCALE * LOG2E) - top)
            ls[h] = ls[h] * back + jnp.sum(w, axis=0, keepdims=True)
            ds[h] = ds[h] * back + jnp.sum(w * dp, axis=0, keepdims=True)
            pb[h, rows, :] = w.astype(bf16)
            db[h, rows, :] = dp.astype(bf16)
            mb[i, h] = top
            ms[h] = top
            top = ahead

    stats(4 + z, True)

    def vy_ready(i, *slots):
        for slot in slots:
            drain(pend["vy", i, slot])

    ring(0, 2)
    ring(1, 2)

    stats_events = {
        0: (lambda: vy_ready(1, 1, 7),),
        1: (lambda: ring(0, 3),),
        2: (lambda: ring(0, 4), lambda: ring(1, 3), lambda: vy_ready(1, 2, 6)),
        3: (lambda: ring(0, 5), lambda: vy_ready(0, *range(8))),
        5: (lambda: ring(1, 4),),
        7: (lambda: vy_ready(1, 3, 5),),
        8: (lambda: ring(1, 5),),
        10: (lambda: vy_ready(1, 4),),
    }
    prompt_at = {3: 0, 5: 1, 6: 2, 8: 3}
    back_at = {0: 1, 1: 7, 2: 2, 4: 6, 7: 3, 9: 5, 10: 4}

    def lookup(table, n, other):
        value = other
        for k, v in table.items():
            value = jnp.where(n == k, v, value)
        return value

    def play(events, n):
        for k, acts in events.items():

            @pl.when(n == k)
            def _():
                for act in acts:
                    act()

    @pl.loop(0, 11)
    def _(n):
        play(stats_events, n)
        chunk = lookup(prompt_at, n, 4 + z - lookup(back_at, n, 0))

        @pl.when((chunk >= 4) | (lookup(prompt_at, n, -1) >= 0))
        def _():
            stats(chunk, False)

    for h in range(HEADS):
        inv = 1.0 / ls[h]
        ls[h] = inv
        ds[h] = ds[h] * inv

    def grads(i):
        rows = aligned(i * KC, KC)
        kt = ks[rows, :].T
        dk = jnp.zeros((KC, D), f32)
        dv = jnp.zeros((KC, D), f32)
        for h in range(HEADS):
            w = pb[h, rows, :].astype(f32) * (jnp.exp2(mb[i, h] - ms[h]) * ls[h])
            d_logit = (w * (db[h, rows, :].astype(f32) - ds[h])).astype(bf16)
            sd[h] = d_logit
            dk = dk + dot(d_logit, qh[h])
            dv = dv + dot(w.astype(bf16), gh[h])
        for h in range(HEADS):
            dqt[h] += dot(kt, sd[h])
        return (dk * SCALE).astype(bf16), dv.astype(bf16)

    kz, vz, vy = {}, {}, {}
    xc = []

    def target(way, far):
        return mod8(z + far) if way == 0 else mod8(z - far)

    def send_vy(slot):
        def parts():
            return dvr.at[mod8(z + slot), 1 - y], v_y.at[slot], yn, rvy_s.at[slot], rvy_r.at[slot]

        vy[slot] = send(("rvy", slot), parts)

    def x_send():
        for dx in range(1, 4):
            for i, src in ((0, dkp), (1, dvp)):

                def parts(dx=dx, i=i, src=src):
                    k = (dx - 1) * 2 + i
                    xx = lax.rem(x + dx, 4)
                    return src.at[:, xx], x_in.at[dx - 1, i], (xx * 2 + y_hi, b), x_s.at[k], x_r.at[k]

                xc.append(send(("x", dx, i), parts))

    def add(ref, index, *terms):
        total = ref[index].astype(f32)
        for term in terms:
            total = total + term.astype(f32)
        ref[index] = total.astype(bf16)

    def k_step(step):
        for way, to in ways:
            t = target(way, 5 - step)
            half = pl.ds(way * 256, 256)

            def parts(way=way, to=to, half=half):
                t = target(way, 5 - step)
                k = way * 4 + step - 1
                src, dst = dkr.at[t], k_in.at[way, step - 1]
                if step == 1:
                    src, dst = dkr.at[t, half], k_in.at[way, 0, half]
                return src, dst, to, rkz_s.at[k], rkz_r.at[k]

            if step == 1:
                kz[way, 1] = send(("rkz", way, 1), parts)
                continue
            kz[way, step - 1].wait_recv()
            if step == 2:
                add(dkr, (t, half), k_in[way, 0, half])
            else:
                add(dkr, (t,), k_in[way, step - 2])
            kz[way, step] = send(("rkz", way, step), parts)

    def v_step(step):
        far = 5 - step
        if step == 1:
            vy[4].wait_recv()
            add(dvr, (mod8(z + 4), y), v_y[4])
        for way, to in ways:
            t = target(way, far)
            half = pl.ds(way * 128, 128)

            def parts(way=way, to=to, half=half):
                t = target(way, far)
                k = way * 4 + step - 1
                src, dst = dvr.at[t, y], v_in.at[way, step - 1]
                if step == 1:
                    src, dst = dvr.at[t, y, half], v_in.at[way, 0, half]
                return src, dst, to, rvz_s.at[k], rvz_r.at[k]

            if step == 1:
                vz[way, 1] = send(("rvz", way, 1), parts)
                continue
            slot = far if way == 0 else 8 - far
            vy[slot].wait_recv()
            vz[way, step - 1].wait_recv()
            if step == 2:
                add(dvr, (t, y), v_y[slot])
                add(dvr, (t, y, half), v_in[way, 0, half])
            else:
                add(dvr, (t, y), v_y[slot], v_in[way, step - 2])
            vz[way, step] = send(("rvz", way, step), parts)

    def yz_copy(o):
        yh, zz, yl = yz_peer(o)
        return pltpu.make_async_remote_copy(
            src_ref=xs.at[:, zz * 2 + yl, aligned(yh * 16, 16), :],
            dst_ref=yz_in.at[o],
            send_sem=yz_s.at[o],
            recv_sem=yz_r.at[o],
            device_id=(x * 2 + yh, zz * 4 + yl * 2 + c),
            device_id_type=MESH,
        )

    def yz_send():
        for copy in xc:
            copy.wait_recv()
        for i, src in ((0, dkp), (1, dvp)):
            xs[i] = (
                src[:, x].astype(f32) + x_in[0, i].astype(f32) + x_in[1, i].astype(f32) + x_in[2, i].astype(f32)
            ).astype(bf16)

        @pl.loop(1, 32)
        def _(o):
            yz_copy(o).start()

    def both(far):
        send_vy(far)
        send_vy(8 - far)

    grads_events = {
        4: (x_send,),
        5: (lambda: k_step(1), lambda: send_vy(4)),
        7: (lambda: both(3), lambda: k_step(2), lambda: v_step(1)),
        9: (lambda: both(2), lambda: k_step(3), lambda: v_step(2)),
        11: (lambda: both(1), lambda: k_step(4), lambda: v_step(3), yz_send),
    }

    @pl.loop(0, 12)
    def _(n):
        play(grads_events, n)
        j = n - 4
        far = 4 - (j + 1) // 2
        t = mod8(jnp.where(lax.rem(j + 8, 2) == 1, z + far, z - far))

        @pl.when((n < 4) | (t <= z))
        def _():
            dk, dv = grads(jnp.where(n < 4, n, 4 + t))

            @pl.when(n < 4)
            def _():
                dkp[pl.ds(n * 4, 4)] = dk.reshape(4, 4, 32, D)
                dvp[pl.ds(n * 4, 4)] = dv.reshape(4, 4, 32, D)

            @pl.when(n >= 4)
            def _():
                dkr[t] = dk
                dvr[t] = dv.reshape(2, 256, D)

    send_vy(0)
    v_step(4)

    dq_copies = []
    for h in range(HEADS):
        dqs[h] = (dqt[h].T * SCALE).astype(bf16)
        to = gq.at[:, aligned(c * 896 + h * D, D)]
        mine = pltpu.make_async_copy(dqs.at[h, aligned(c * 128, 128), :], to, dq_own.at[h])
        mine.start()
        theirs = send(
            ("dq", h),
            lambda h=h, to=to: (dqs.at[h, aligned((1 - c) * 128, 128), :], to, sib, dq_s.at[h], dq_r.at[h]),
        )
        dq_copies.append((mine, theirs))

    yz_in[0] = xs[:, p, aligned(y_hi * 16, 16), :]

    @pl.loop(1, 32)
    def _(o):
        yz_copy(o).wait()

    g_out[...] = jnp.sum(yz_in[...].astype(f32), axis=0).astype(bf16)
    core = r // 4
    part = lax.rem(r, 4)
    for i, out in ((0, pkg), (1, pvg)):
        for o in range(8):
            src = g_out.at[i]
            dst = out.at[aligned(part * 16, 16), aligned(c * 128, 128)]
            s_sem, r_sem = g_s.at[i * 8 + o], g_r.at[i * 8 + part * 2 + c]
            to = (lax.rem(r + o, 8), p * 2 + core)
            if o == 0:

                @pl.when(core == c)
                def _():
                    pltpu.make_async_copy(src, dst, r_sem).start()

                @pl.when(core != c)
                def _():
                    pltpu.make_async_remote_copy(
                        src_ref=src, dst_ref=dst, send_sem=s_sem, recv_sem=r_sem, device_id=to, device_id_type=MESH
                    ).start()
            else:
                send(("g", i, o), lambda a=(src, dst, to, s_sem, r_sem): a)

    for way in (0, 1):
        kz[way, 4].wait_recv()
    total = dkr[z].astype(f32) + k_in[0, 3].astype(f32) + k_in[1, 3].astype(f32)
    ky_out[...] = total.astype(bf16).reshape(2, 256, D)
    ky = send(("rky",), lambda: (ky_out.at[1 - y], ky_in, yn, rky_s, rky_r))

    vy[0].wait_recv()
    for way in (0, 1):
        vz[way, 4].wait_recv()
    fin[1] = (
        dvr[z, y].astype(f32) + v_y[0].astype(f32) + v_in[0, 3].astype(f32) + v_in[1, 3].astype(f32)
    ).astype(bf16)
    lines = aligned(y * 256, 256)
    ky.wait_recv()
    fin[0] = (
        dkr[z, lines].astype(f32) + k_in[0, 3, lines].astype(f32) + k_in[1, 3, lines].astype(f32)
        + ky_in[...].astype(f32)
    ).astype(bf16)
    last = []
    for i, out in ((0, gk), (1, gv)):
        to = out.at[:, aligned(c * 128, 128)]
        mine = pltpu.make_async_copy(fin.at[i, aligned(c * 128, 128), :], to, f_sem.at[i])
        mine.start()
        theirs = send(
            ("fin", i),
            lambda i=i, to=to: (fin.at[i, aligned((1 - c) * 128, 128), :], to, sib, f_sem.at[2 + i], f_sem.at[4 + i]),
        )
        last.append((mine, theirs))
    for mine, theirs in last + dq_copies:
        mine.wait()
        theirs.wait_recv()
    for i, out in ((0, pkg), (1, pvg)):
        for k in range(8):
            pltpu.make_async_copy(g_out.at[i], out.at[0:16, 0:128], g_r.at[i * 8 + k]).wait()

        @pl.when(core != c)
        def _():
            pltpu.make_async_copy(g_out.at[i], out.at[0:16, 0:128], g_s.at[i * 8]).wait()

    for copy in sent.values():
        copy.wait_send()


def hand_on_kernel(*refs):
    ins, outs, held, sems = refs[:5], refs[5:10], refs[10:15], refs[15]
    loads = [pltpu.make_async_copy(ins[i], held[i], sems.at[i]) for i in range(5)]
    stores = [pltpu.make_async_copy(held[i], outs[i], sems.at[5 + i]) for i in range(5)]
    for copy in loads:
        copy.start()
    for load, store in zip(loads, stores):
        load.wait()
        store.start()
    for copy in stores:
        copy.wait()


def shards(q, rk, rv, pk, pv, go, lengths):
    rows = q.shape[1]
    dma = pltpu.SemaphoreType.DMA
    n_keys = PROMPT + RESP

    def out(*shape):
        return jax.ShapeDtypeStruct(shape, bf16)

    def v(*shape, dtype=bf16):
        return pltpu.VMEM(shape, dtype)

    def w(*shape):
        return pltpu.VMEM(shape, f32)

    outs = pl.pallas_call(
        fused_kernel,
        out_shape=(out(rows, 1792), out(rows, 256), out(rows, 256), out(64, 256), out(64, 256)),
        in_specs=[SMEM] + [ANY] * 6,
        out_specs=(ANY,) * 5,
        scratch_shapes=[
            v(HEADS, 256, D), v(HEADS, 256, D), v(HEADS, D, 256), v(HEADS, D, 256), v(n_keys, D), v(n_keys, D),
            v(HEADS, n_keys, 256), v(HEADS, n_keys, 256), w(n_keys // KC, HEADS, 1, 256),
            w(HEADS, 1, 256), w(HEADS, 1, 256), w(HEADS, 1, 256), w(HEADS, 1, 256),
            w(2, KC, 256), v(HEADS, KC, 256), w(HEADS, D, 256), v(HEADS, 256, D),
            v(8, 512, D), v(8, 2, 256, D), v(16, 4, 32, D), v(16, 4, 32, D),
            v(2, 4, 512, D), v(2, 4, 256, D), v(8, 256, D), v(2, 256, D), v(256, D), v(2, 256, D),
            v(3, 2, 16, 32, D), v(2, 16, 32, D), v(32, 2, 16, D), v(2, 16, D),
            dma((4,)), dma((4,)), dma((4,)), dma((14,)), dma((14,)), dma((14,)),
            dma((2,)), dma((2,)), dma((16,)), dma((16,)), dma((16,)), dma((16,)), dma((16,)), dma((16,)),
            dma((8,)), dma((8,)), dma((8,)), dma((8,)), dma((8,)), dma((8,)), dma, dma, dma((6,)),
            dma((6,)), dma((6,)), dma((32,)), dma((32,)), dma((16,)), dma((16,)), dma((7,)), dma((7,)), dma((7,)),
        ],
        compiler_params=pltpu.CompilerParams(
            collective_id=0, has_side_effects=True, vmem_limit_bytes=63 * 2**20
        ),
        name="fused",
    )(lengths, q[0], go[0], rk[0], rv[0], pk, pv)
    gq, gk, gv, pkg, pvg = pl.pallas_call(
        hand_on_kernel,
        out_shape=tuple(jax.ShapeDtypeStruct(x.shape, x.dtype) for x in outs),
        in_specs=[ANY] * 5,
        out_specs=(ANY,) * 5,
        scratch_shapes=[v(*x.shape) for x in outs] + [dma((10,))],
        compiler_params=pltpu.CompilerParams(vmem_limit_bytes=63 * 2**20),
        name="hand_on",
    )(*outs)
    return gq[None], gk[None], gv[None], pkg, pvg


def solution(mesh):
    in_specs = (
        P("resp", "blk", None),
        P("resp", "blk", None),
        P("resp", "blk", None),
        P("blk", None),
        P("blk", None),
        P("resp", "blk", None),
        P("resp"),
    )
    out_specs = (
        P("resp", "blk", None),
        P("resp", "blk", None),
        P("resp", "blk", None),
        P("blk", None),
        P("blk", None),
    )
    return jax.shard_map(shards, mesh=mesh, in_specs=in_specs, out_specs=out_specs, check_vma=False)
```

```python
import functools

import jax
import jax.numpy as jnp
from jax import lax
from jax.experimental import pallas as pl
from jax.experimental.pallas import tpu as pltpu
from jax.sharding import PartitionSpec as P

HEADS = 7
D = 128
RESP = 4096
PROMPT = 2048
PBLOCKS = PROMPT // 128
SCALE = D**-0.5
LOG2E = 1.4426950408889634
KC = 512
f32, bf16 = jnp.float32, jnp.bfloat16
MESH = pl.DeviceIdType.MESH
ANY = pl.BlockSpec(memory_space=pl.ANY)
VMEM = pl.BlockSpec(memory_space=pltpu.VMEM)
SMEM = pl.BlockSpec(memory_space=pltpu.SMEM)


def dot(a, b):
    return jnp.dot(a, b, preferred_element_type=f32)


def place():
    r, b = lax.axis_index("resp"), lax.axis_index("blk")
    z, y, c = b // 4, lax.rem(b // 2, 2), lax.rem(b, 2)
    return r, b, z, y, c


def aligned(start, size):
    return pl.ds(pl.multiple_of(start, size), size)


def mod8(value):
    return lax.rem(value + 16, 8)


class Remote:
    def __init__(self, parts):
        self.parts = parts

    def make(self):
        src, dst, to, s_sem, r_sem = self.parts()
        return pltpu.make_async_remote_copy(
            src_ref=src, dst_ref=dst, send_sem=s_sem, recv_sem=r_sem, device_id=to, device_id_type=MESH
        )

    def start(self):
        self.make().start()

    def wait_recv(self):
        self.make().wait_recv()

    def wait_send(self):
        self.make().wait_send()


def fused_kernel(
    length, q, g, rk, rv, pk, pv, gq, gkv, pgkv,
    qh, gh, qt, gt, kv, shard, pb, db, mb, ms, ls, ds, cen, sb, sd, dqt, dqs,
    dkr, dvr, dp_kv, k_in, v_in, v_y, ky_out, ky_in, fin, x_in, xs, yz_in, g_out,
    own_sem, sib_s, sib_r, qg_own, qg_s, qg_r,
    ky_s, ky_r, rz_s, rz_r, vy_s, vy_r, pz_s, pz_r, px_s, px_r,
    rkz_s, rkz_r, rvz_s, rvz_r, rvy_s, rvy_r, rky_s, rky_r, f_sem,
    x_s, x_r, yz_s, yz_r, g_s, g_r, dq_own, dq_s, dq_r,
):
    r, b, z, y, c = place()
    x, y_hi = r // 2, lax.rem(r, 2)
    p = z * 2 + y
    ks, vs = kv.at[0], kv.at[1]
    sib = (r, b + 1 - 2 * c)
    yn = (r, b + 2 - 4 * y)
    zr = (r, lax.rem(b + 4, 32))
    zl = (r, lax.rem(b + 28, 32))
    ways = ((0, zr), (1, zl))

    def yz_peer(o):
        yh = lax.rem(y_hi + o // 16, 2)
        zz = lax.rem(z + lax.rem(o // 2, 8), 8)
        yl = lax.rem(y + lax.rem(o, 2), 2)
        return yh, zz, yl

    sem = pltpu.get_barrier_semaphore()

    @pl.loop(1, 32)
    def _(o):
        yh, zz, yl = yz_peer(o)
        pl.semaphore_signal(sem, inc=1, device_id=(x * 2 + yh, zz * 4 + yl * 2 + c), device_id_type=MESH)

    @pl.loop(1, 16)
    def _(o):
        rr = lax.rem(r + o // 2, 8)
        cc = lax.rem(c + lax.rem(o, 2), 2)
        pl.semaphore_signal(sem, inc=1, device_id=(rr, p * 2 + cc), device_id_type=MESH)

    kv_parts = (
        (pk, shard.at[0], lambda ref: ref.at[aligned(c * 2, 2)]),
        (pv, shard.at[1], lambda ref: ref.at[aligned(c * 2, 2)]),
        (rk, ks, lambda ref: ref.at[PBLOCKS + p * 2 + c]),
        (rv, vs, lambda ref: ref.at[PBLOCKS + p * 2 + c]),
    )
    qg_parts = [(i, h) for i in range(2) for h in range(HEADS)]
    own = []
    for i, (src, dst, part) in enumerate(kv_parts):
        own.append(pltpu.make_async_copy(src.at[:, :, aligned(c * D, D)], part(dst), own_sem.at[i]))
    for i, h in qg_parts:
        src, dst = ((q, qh), (g, gh))[i]
        own.append(
            pltpu.make_async_copy(
                src.at[:, aligned(c * 896 + h * D, D)],
                dst.at[h, aligned(c * 128, 128), :],
                qg_own.at[i * HEADS + h],
            )
        )
    for copy in own:
        copy.start()
    dkr[...] = jnp.zeros_like(dkr)
    dvr[...] = jnp.zeros_like(dvr)
    dqt[...] = jnp.zeros_like(dqt)
    ms[...] = jnp.full_like(ms, -1e30)
    ls[...] = jnp.zeros_like(ls)
    ds[...] = jnp.zeros_like(ds)
    for copy in own:
        copy.wait()

    def half_ready(half):
        rows = aligned(half * 128, 128)
        keep = lax.broadcasted_iota(jnp.int32, (128, D), 0) + (p * 256 + half * 128) < length[0]
        for h in range(HEADS):
            part = jnp.where(keep, gh[h, rows, :].astype(f32), 0.0).astype(bf16)
            gh[h, rows, :] = part
            gt[h, :, rows] = part.T
            qt[h, :, rows] = qh[h, rows, :].T

    half_ready(c)
    pl.semaphore_wait(sem, 46)
    sent = {}

    def send(key, parts):
        copy = Remote(parts)
        copy.start()
        sent[key] = copy
        return copy

    def drain(pending):
        for copy in pending:
            copy.wait_recv()

    swaps, qg_swaps = [], []
    for i, (src, dst, part) in enumerate(kv_parts):

        def parts(i=i, src=src, dst=dst, part=part):
            return src.at[:, :, aligned((1 - c) * D, D)], part(dst), sib, sib_s.at[i], sib_r.at[i]

        swaps.append(send(("kv", i), parts))
    for i, h in qg_parts:

        def parts(i=i, h=h):
            src, dst = ((q, qh), (g, gh))[i]
            k = i * HEADS + h
            col = aligned((1 - c) * 896 + h * D, D)
            return src.at[:, col], dst.at[h, aligned(c * 128, 128), :], sib, qg_s.at[k], qg_r.at[k]

        qg_swaps.append(send(("qg", i, h), parts))
    for copy in swaps:
        copy.wait_recv()
    kv[:, p, x] = shard[:, x]

    def zy_peer(o):
        return lax.rem(z + o // 2, 8), lax.rem(y + lax.rem(o, 2), 2)

    def piece_copy(o):
        zz, yl = zy_peer(o)
        return pltpu.make_async_remote_copy(
            src_ref=shard.at[:, x],
            dst_ref=kv.at[:, p, x],
            send_sem=pz_s.at[o],
            recv_sem=pz_r.at[o],
            device_id=(r, zz * 4 + yl * 2 + c),
            device_id_type=MESH,
        )

    streams = {"v": (0, vs, y), "k": (1, ks, y), "kb": (2, ks, 1 - y)}
    pend = {}

    def block(t, line):
        return PBLOCKS + (t * 2 + line) * 2

    def push(key, ref, span, to, s_sems, r_sems, k):
        def parts():
            start, size = span()
            part = ref.at[pl.ds(start, size)]
            return part, part, to, s_sems.at[k], r_sems.at[k]

        return send(key, parts)

    def start_z(name, step):
        number, ref, line = streams[name]
        out = []
        for way, to in ways:

            def span(way=way):
                t = mod8(z - step + 1) if way == 0 else mod8(z + step - 1)
                return (block(t, line) + way, 1) if step == 4 else (block(t, line), 2)

            k = number * 8 + way * 4 + step - 1
            out.append(push(("z", k), ref, span, to, rz_s, rz_r, k))
        pend[name, step] = out

    def start_vy(slot):
        def span():
            return block(mod8(z - slot), y), 2

        pend["vy", slot] = [push(("vy", slot), vs, span, yn, vy_s, vy_r, slot)]

    def ring(step):
        for name in ("v", "k", "kb"):
            drain(pend[name, step - 1])
            if step < 5:
                start_z(name, step)
            if name == "v":
                start_vy(step - 1)
                if step < 5:
                    start_vy(9 - step)

    pend["ky"] = [push(("ky",), ks, lambda: (block(z, y), 2), yn, ky_s, ky_r, 0)]
    start_z("v", 1)
    start_z("k", 1)
    start_vy(0)

    @pl.loop(1, 16)
    def _(o):
        piece_copy(o).start()

    drain(pend["ky"])
    start_z("kb", 1)
    for copy in qg_swaps:
        copy.wait_recv()
    half_ready(1 - c)
    drain(pend["vy", 0])
    middle = jnp.mean(vs[aligned(PBLOCKS + z * 4, 4)].reshape(KC, D).astype(f32), axis=0, keepdims=True)
    middle = jnp.broadcast_to(middle, (16, D)).astype(bf16)
    for h in range(HEADS):
        cen[h] = dot(middle, gt[h])[0:1]

    def stats(i, masked):
        rows = aligned(i * KC, KC)
        kc = ks[aligned(i * 4, 4)].reshape(KC, D)
        vc = vs[aligned(i * 4, 4)].reshape(KC, D)

        def logits(h):
            s = dot(kc, qt[h])
            if masked:
                key = lax.broadcasted_iota(jnp.int32, s.shape, 0)
                pos = lax.broadcasted_iota(jnp.int32, s.shape, 1) + y * 256
                s = jnp.where(key <= pos, s, -jnp.inf)
            sb[h % 2] = s
            return jnp.maximum(ms[h], jnp.max(s, axis=0, keepdims=True) * (SCALE * LOG2E))

        top = logits(0)
        for h in range(HEADS):
            ahead = logits(h + 1) if h + 1 < HEADS else None
            dp = dot(vc, gt[h]) - cen[h]
            back = jnp.exp2(ms[h] - top)
            w = jnp.exp2(sb[h % 2] * (SCALE * LOG2E) - top)
            ls[h] = ls[h] * back + jnp.sum(w, axis=0, keepdims=True)
            ds[h] = ds[h] * back + jnp.sum(w * dp, axis=0, keepdims=True)
            pb[h, rows, :] = w.astype(bf16)
            db[h, rows, :] = dp.astype(bf16)
            mb[i, h] = top
            ms[h] = top
            top = ahead

    stats(4 + z, True)

    def vy_ready(*slots):
        for slot in slots:
            drain(pend["vy", slot])

    ring(2)

    @pl.loop(1, 16)
    def _(o):
        piece_copy(o).wait()

    for half in range(2):
        pend["px", half] = []
        for dx in range(1, 4):

            def parts(half=half, dx=dx):
                k = half * 3 + dx - 1
                part = kv.at[:, pl.ds(half * 8, 8), x]
                return part, part, (lax.rem(x + dx, 4) * 2 + y_hi, b), px_s.at[k], px_r.at[k]

            pend["px", half].append(send(("px", half, dx), parts))

    stats_events = {
        0: (lambda: vy_ready(1, 7),),
        2: (lambda: ring(3), lambda: vy_ready(2, 6)),
        4: (lambda: ring(4), lambda: drain(pend["px", 0])),
        6: (lambda: vy_ready(3, 5),),
        8: (lambda: ring(5), lambda: vy_ready(4)),
        9: (lambda: drain(pend["px", 1]),),
    }
    prompt_at = {4: 0, 5: 1, 9: 2, 10: 3}
    back_at = {0: 1, 1: 7, 2: 2, 3: 6, 6: 3, 7: 5, 8: 4}

    def lookup(table, n, other):
        value = other
        for k, v in table.items():
            value = jnp.where(n == k, v, value)
        return value

    def play(events, n):
        for k, acts in events.items():

            @pl.when(n == k)
            def _():
                for act in acts:
                    act()

    @pl.loop(0, 11)
    def _(n):
        play(stats_events, n)
        chunk = lookup(prompt_at, n, 4 + z - lookup(back_at, n, 0))

        @pl.when((chunk >= 4) | (lookup(prompt_at, n, -1) >= 0))
        def _():
            stats(chunk, False)

    for h in range(HEADS):
        inv = 1.0 / ls[h]
        ls[h] = inv
        ds[h] = ds[h] * inv

    def grads(i):
        rows = aligned(i * KC, KC)
        kt = ks[aligned(i * 4, 4)].reshape(KC, D).T
        dk = jnp.zeros((KC, D), f32)
        dv = jnp.zeros((KC, D), f32)
        for h in range(HEADS):
            w = pb[h, rows, :].astype(f32) * (jnp.exp2(mb[i, h] - ms[h]) * ls[h])
            d_logit = (w * (db[h, rows, :].astype(f32) - ds[h])).astype(bf16)
            sd[h] = d_logit
            dk = dk + dot(d_logit, qh[h])
            dv = dv + dot(w.astype(bf16), gh[h])
        for h in range(HEADS):
            dqt[h] += dot(kt, sd[h])
        return (dk * SCALE).astype(bf16), dv.astype(bf16)

    kz, vz, vy = {}, {}, {}
    xc = []

    def target(way, far):
        return mod8(z + far) if way == 0 else mod8(z - far)

    def sends(way, step, zz):
        ahead = zz + 5 - step
        return (ahead >= 8) | (ahead <= 3) if way == 0 else zz >= 5 - step

    def receives(way, step):
        return sends(way, step, mod8(z - 1) if way == 0 else mod8(z + 1))

    def sees(slot):
        return mod8(z + slot) <= z

    def send_if(key, condition, parts):
        copy = Remote(parts)
        pl.when(condition())(copy.start)
        maybe_sent[key] = (condition, copy)
        return copy

    maybe_sent = {}

    def send_vy(slot):
        def parts():
            return dvr.at[mod8(z + slot), 1 - y], v_y.at[slot], yn, rvy_s.at[slot], rvy_r.at[slot]

        vy[slot] = send_if(("rvy", slot), lambda: sees(slot), parts)

    def wait_vy(slot, ref_index):
        @pl.when(sees(slot))
        def _():
            vy[slot].wait_recv()
            add(dvr, ref_index, v_y[slot])

    def x_send(half):
        for dx in range(1, 4):

            def parts(dx=dx):
                k = half * 3 + dx - 1
                span = pl.ds(half * 8, 8)
                xx = lax.rem(x + dx, 4)
                return dp_kv.at[:, span, xx], x_in.at[dx - 1, :, span], (xx * 2 + y_hi, b), x_s.at[k], x_r.at[k]

            xc.append(send(("x", half, dx), parts))

    def add(ref, index, *terms):
        total = ref[index].astype(f32)
        for term in terms:
            total = total + term.astype(f32)
        ref[index] = total.astype(bf16)

    k_lines = (1 - y, y)

    def k_step(step):
        for stream, line in enumerate(k_lines):
            for way, to in ways:
                t = target(way, 5 - step)
                half = pl.ds(way * 128, 128)

                def parts(stream=stream, line=line, way=way, to=to, half=half):
                    t = target(way, 5 - step)
                    k = stream * 8 + way * 4 + step - 1
                    src, dst = dkr.at[t, line], k_in.at[stream, way, step - 1]
                    if step == 1:
                        src, dst = dkr.at[t, line, half], k_in.at[stream, way, 0, half]
                    return src, dst, to, rkz_s.at[k], rkz_r.at[k]

                if step > 1:

                    @pl.when(receives(way, step - 1))
                    def _():
                        kz[stream, way, step - 1].wait_recv()
                        if step == 2:
                            add(dkr, (t, line, half), k_in[stream, way, 0, half])
                        else:
                            add(dkr, (t, line), k_in[stream, way, step - 2])

                kz[stream, way, step] = send_if(
                    ("rkz", stream, way, step), lambda way=way: sends(way, step, z), parts
                )

    def v_step(step):
        far = 5 - step
        if step == 1:
            wait_vy(4, (mod8(z + 4), y))
        for way, to in ways:
            t = target(way, far)
            half = pl.ds(way * 128, 128)

            def parts(way=way, to=to, half=half):
                t = target(way, far)
                k = way * 4 + step - 1
                src, dst = dvr.at[t, y], v_in.at[way, step - 1]
                if step == 1:
                    src, dst = dvr.at[t, y, half], v_in.at[way, 0, half]
                return src, dst, to, rvz_s.at[k], rvz_r.at[k]

            if step > 1:
                wait_vy(far if way == 0 else 8 - far, (t, y))

                @pl.when(receives(way, step - 1))
                def _():
                    vz[way, step - 1].wait_recv()
                    if step == 2:
                        add(dvr, (t, y, half), v_in[way, 0, half])
                    else:
                        add(dvr, (t, y), v_in[way, step - 2])

            vz[way, step] = send_if(("rvz", way, step), lambda way=way: sends(way, step, z), parts)

    def yz_copy(o):
        yh, zz, yl = yz_peer(o)
        return pltpu.make_async_remote_copy(
            src_ref=xs.at[:, zz * 2 + yl, aligned(yh * 16, 16), :],
            dst_ref=yz_in.at[o],
            send_sem=yz_s.at[o],
            recv_sem=yz_r.at[o],
            device_id=(x * 2 + yh, zz * 4 + yl * 2 + c),
            device_id_type=MESH,
        )

    def yz_send():
        for copy in xc:
            copy.wait_recv()
        for i in range(2):
            xs[i] = (
                dp_kv[i, :, x].astype(f32) + x_in[0, i].astype(f32) + x_in[1, i].astype(f32) + x_in[2, i].astype(f32)
            ).astype(bf16)

        @pl.loop(1, 32)
        def _(o):
            yz_copy(o).start()

    def both(far):
        send_vy(far)
        send_vy(8 - far)

    grads_events = {
        1: (lambda: k_step(1), lambda: send_vy(4)),
        3: (lambda: both(3),),
        4: (lambda: v_step(1),),
        5: (lambda: x_send(0), lambda: k_step(2)),
        7: (lambda: x_send(1), lambda: v_step(2)),
        9: (lambda: both(2), lambda: k_step(3)),
        11: (lambda: both(1),),
    }
    ahead_at = {0: 4, 1: 3, 2: 5, 7: 2, 8: 6, 9: 1, 10: 7, 11: 0}
    prompt_now = {3: 0, 4: 1, 5: 2, 6: 3}

    @pl.loop(0, 12)
    def _(n):
        play(grads_events, n)
        t = mod8(z + lookup(ahead_at, n, 0))
        is_prompt = (n >= 3) & (n <= 6)

        @pl.when(is_prompt | (t <= z))
        def _():
            chunk = lookup(prompt_now, n, 4 + t)
            dk, dv = grads(chunk)

            @pl.when(is_prompt)
            def _():
                dp_kv[0, pl.ds(chunk * 4, 4)] = dk.reshape(4, 4, 32, D)
                dp_kv[1, pl.ds(chunk * 4, 4)] = dv.reshape(4, 4, 32, D)

            @pl.when(jnp.logical_not(is_prompt))
            def _():
                dkr[t] = dk.reshape(2, 256, D)
                dvr[t] = dv.reshape(2, 256, D)

    send_vy(0)
    k_step(4)
    v_step(3)

    dq_copies = []
    for h in range(HEADS):
        dqs[h] = (dqt[h].T * SCALE).astype(bf16)
        to = gq.at[:, aligned(c * 896 + h * D, D)]
        mine = pltpu.make_async_copy(dqs.at[h, aligned(c * 128, 128), :], to, dq_own.at[h])
        mine.start()
        theirs = send(
            ("dq", h),
            lambda h=h, to=to: (dqs.at[h, aligned((1 - c) * 128, 128), :], to, sib, dq_s.at[h], dq_r.at[h]),
        )
        dq_copies.append((mine, theirs))
    yz_send()
    v_step(4)

    def last_terms(copies, ref, index, ins):
        for way in (0, 1):

            @pl.when(receives(way, 4))
            def _():
                copies(way).wait_recv()
                add(ref, index, ins(way))

    last_terms(lambda way: kz[0, way, 4], dkr, (z, 1 - y), lambda way: k_in[0, way, 3])
    ky_out[...] = dkr[z, 1 - y]
    ky = send(("rky",), lambda: (ky_out, ky_in, yn, rky_s, rky_r))

    yz_in[0] = xs[:, p, aligned(y_hi * 16, 16), :]

    @pl.loop(1, 32)
    def _(o):
        yz_copy(o).wait()

    g_out[...] = jnp.sum(yz_in[...].astype(f32), axis=0).astype(bf16)
    core = r // 4
    part = lax.rem(r, 4)
    for o in range(8):
        dst = pgkv.at[:, aligned(part * 16, 16), aligned(c * 128, 128)]
        s_sem, r_sem = g_s.at[o], g_r.at[part * 2 + c]
        to = (lax.rem(r + o, 8), p * 2 + core)
        if o == 0:

            @pl.when(core == c)
            def _():
                pltpu.make_async_copy(g_out, dst, r_sem).start()

            @pl.when(core != c)
            def _():
                pltpu.make_async_remote_copy(
                    src_ref=g_out, dst_ref=dst, send_sem=s_sem, recv_sem=r_sem, device_id=to, device_id_type=MESH
                ).start()
        else:
            send(("g", o), lambda a=(g_out, dst, to, s_sem, r_sem): a)

    last = []

    def finish(i, out):
        to = out.at[:, aligned(c * 128, 128)]
        mine = pltpu.make_async_copy(fin.at[i, aligned(c * 128, 128), :], to, f_sem.at[i])
        mine.start()
        theirs = send(
            ("fin", i),
            lambda: (fin.at[i, aligned((1 - c) * 128, 128), :], to, sib, f_sem.at[2 + i], f_sem.at[4 + i]),
        )
        last.append((mine, theirs))

    wait_vy(0, (z, y))
    last_terms(lambda way: vz[way, 4], dvr, (z, y), lambda way: v_in[way, 3])
    fin[1] = dvr[z, y]
    finish(1, gkv.at[1])
    last_terms(lambda way: kz[1, way, 4], dkr, (z, y), lambda way: k_in[1, way, 3])
    ky.wait_recv()
    fin[0] = (dkr[z, y].astype(f32) + ky_in[...].astype(f32)).astype(bf16)
    finish(0, gkv.at[0])
    for mine, theirs in last + dq_copies:
        mine.wait()
        theirs.wait_recv()
    for k in range(8):
        pltpu.make_async_copy(g_out, pgkv.at[:, 0:16, 0:128], g_r.at[k]).wait()

    @pl.when(core != c)
    def _():
        pltpu.make_async_copy(g_out, pgkv.at[:, 0:16, 0:128], g_s.at[0]).wait()

    for copy in sent.values():
        copy.wait_send()
    for condition, copy in maybe_sent.values():
        pl.when(condition())(copy.wait_send)


def hand_on_kernel(gq, gkv, pgkv, out_q, out_k, out_v, out_pk, out_pv, *held_and_sems):
    held, sems = held_and_sems[:5], held_and_sems[5]
    ins = (gq, gkv.at[0], gkv.at[1], pgkv.at[0], pgkv.at[1])
    outs = (out_q, out_k, out_v, out_pk, out_pv)
    loads = [pltpu.make_async_copy(ins[i], held[i], sems.at[i]) for i in range(5)]
    stores = [pltpu.make_async_copy(held[i], outs[i], sems.at[5 + i]) for i in range(5)]
    for copy in loads:
        copy.start()
    for load, store in zip(loads, stores):
        load.wait()
        store.start()
    for copy in stores:
        copy.wait()


def shards(q, rk, rv, pk, pv, go, lengths):
    rows = q.shape[1]
    dma = pltpu.SemaphoreType.DMA
    n_keys = PROMPT + RESP

    def out(*shape):
        return jax.ShapeDtypeStruct(shape, bf16)

    def v(*shape, dtype=bf16):
        return pltpu.VMEM(shape, dtype)

    def w(*shape):
        return pltpu.VMEM(shape, f32)

    outs = pl.pallas_call(
        fused_kernel,
        out_shape=(out(rows, 1792), out(2, rows, 256), out(2, 64, 256)),
        in_specs=[SMEM] + [ANY] * 6,
        out_specs=(ANY,) * 3,
        scratch_shapes=[
            v(HEADS, 256, D), v(HEADS, 256, D), v(HEADS, D, 256), v(HEADS, D, 256),
            v(2, n_keys // 128, 4, 32, D), v(2, 4, 32, D),
            v(HEADS, n_keys, 256), v(HEADS, n_keys, 256), w(n_keys // KC, HEADS, 1, 256),
            w(HEADS, 1, 256), w(HEADS, 1, 256), w(HEADS, 1, 256), w(HEADS, 1, 256),
            w(2, KC, 256), v(HEADS, KC, 256), w(HEADS, D, 256), v(HEADS, 256, D),
            v(8, 2, 256, D), v(8, 2, 256, D), v(2, 16, 4, 32, D),
            v(2, 2, 4, 256, D), v(2, 4, 256, D), v(8, 256, D), v(256, D), v(256, D), v(2, 256, D),
            v(3, 2, 16, 32, D), v(2, 16, 32, D), v(32, 2, 16, D), v(2, 16, D),
            dma((4,)), dma((4,)), dma((4,)), dma((14,)), dma((14,)), dma((14,)),
            dma((1,)), dma((1,)), dma((24,)), dma((24,)), dma((8,)), dma((8,)),
            dma((16,)), dma((16,)), dma((6,)), dma((6,)),
            dma((16,)), dma((16,)), dma((8,)), dma((8,)), dma((8,)), dma((8,)), dma, dma, dma((6,)),
            dma((6,)), dma((6,)), dma((32,)), dma((32,)), dma((8,)), dma((8,)), dma((7,)), dma((7,)), dma((7,)),
        ],
        compiler_params=pltpu.CompilerParams(
            collective_id=0, has_side_effects=True, vmem_limit_bytes=63 * 2**20
        ),
        name="fused",
    )(
        lengths, q[0], go[0], rk[0].reshape(4, 32, 256), rv[0].reshape(4, 32, 256),
        pk.reshape(2, 32, 256), pv.reshape(2, 32, 256),
    )
    results = ((rows, 1792), (rows, 256), (rows, 256), (64, 256), (64, 256))
    gq, gk, gv, pkg, pvg = pl.pallas_call(
        hand_on_kernel,
        out_shape=tuple(out(*shape) for shape in results),
        in_specs=[ANY] * 3,
        out_specs=(ANY,) * 5,
        scratch_shapes=[v(*shape) for shape in results] + [dma((10,))],
        compiler_params=pltpu.CompilerParams(vmem_limit_bytes=63 * 2**20),
        name="hand_on",
    )(*outs)
    return gq[None], gk[None], gv[None], pkg, pvg


def solution(mesh):
    in_specs = (
        P("resp", "blk", None),
        P("resp", "blk", None),
        P("resp", "blk", None),
        P("blk", None),
        P("blk", None),
        P("resp", "blk", None),
        P("resp"),
    )
    out_specs = (
        P("resp", "blk", None),
        P("resp", "blk", None),
        P("resp", "blk", None),
        P("blk", None),
        P("blk", None),
    )
    return jax.shard_map(shards, mesh=mesh, in_specs=in_specs, out_specs=out_specs, check_vma=False)
```

```python
import functools

import jax
import jax.numpy as jnp
from jax import lax
from jax.experimental import pallas as pl
from jax.experimental.pallas import tpu as pltpu
from jax.sharding import PartitionSpec as P

HEADS = 7
D = 128
RESP = 4096
PROMPT = 2048
PBLOCKS = PROMPT // 128
SCALE = D**-0.5
LOG2E = 1.4426950408889634
KC = 512
f32, bf16 = jnp.float32, jnp.bfloat16
MESH = pl.DeviceIdType.MESH
ANY = pl.BlockSpec(memory_space=pl.ANY)
VMEM = pl.BlockSpec(memory_space=pltpu.VMEM)
SMEM = pl.BlockSpec(memory_space=pltpu.SMEM)


def dot(a, b):
    return jnp.dot(a, b, preferred_element_type=f32)


def place():
    r, b = lax.axis_index("resp"), lax.axis_index("blk")
    z, y, c = b // 4, lax.rem(b // 2, 2), lax.rem(b, 2)
    return r, b, z, y, c


def aligned(start, size):
    return pl.ds(pl.multiple_of(start, size), size)


def mod8(value):
    return lax.rem(value + 16, 8)


class Remote:
    def __init__(self, parts):
        self.parts = parts

    def make(self):
        src, dst, to, s_sem, r_sem = self.parts()
        return pltpu.make_async_remote_copy(
            src_ref=src, dst_ref=dst, send_sem=s_sem, recv_sem=r_sem, device_id=to, device_id_type=MESH
        )

    def start(self):
        self.make().start()

    def wait_recv(self):
        self.make().wait_recv()

    def wait_send(self):
        self.make().wait_send()


def fused_kernel(
    length, q, g, rk, rv, pk, pv, gq, gkv, pgkv,
    qh, gh, qt, gt, kv, shard, pb, db, mb, ms, ls, ds, cen, sb, sd, dqt, dqs,
    dkr, dvr, dp_kv, k_in, v_in, v_y, ky_out, ky_in, fin, x_in, xs, yz_in, g_out,
    own_sem, sib_s, sib_r, qg_own, qg_s, qg_r,
    ky_s, ky_r, rz_s, rz_r, vy_s, vy_r, pz_s, pz_r, px_s, px_r,
    rkz_s, rkz_r, rvz_s, rvz_r, rvy_s, rvy_r, rky_s, rky_r, f_sem,
    x_s, x_r, yz_s, yz_r, g_s, g_r, dq_own, dq_s, dq_r,
):
    r, b, z, y, c = place()
    x, y_hi = r // 2, lax.rem(r, 2)
    p = z * 2 + y
    ks, vs = kv.at[0], kv.at[1]
    sib = (r, b + 1 - 2 * c)
    yn = (r, b + 2 - 4 * y)
    zr = (r, lax.rem(b + 4, 32))
    zl = (r, lax.rem(b + 28, 32))
    ways = ((0, zr), (1, zl))

    def yz_peer(o):
        yh = lax.rem(y_hi + o // 16, 2)
        zz = lax.rem(z + lax.rem(o // 2, 8), 8)
        yl = lax.rem(y + lax.rem(o, 2), 2)
        return yh, zz, yl

    sem = pltpu.get_barrier_semaphore()

    @pl.loop(1, 32)
    def _(o):
        yh, zz, yl = yz_peer(o)
        pl.semaphore_signal(sem, inc=1, device_id=(x * 2 + yh, zz * 4 + yl * 2 + c), device_id_type=MESH)

    @pl.loop(1, 16)
    def _(o):
        rr = lax.rem(r + o // 2, 8)
        cc = lax.rem(c + lax.rem(o, 2), 2)
        pl.semaphore_signal(sem, inc=1, device_id=(rr, p * 2 + cc), device_id_type=MESH)

    kv_parts = (
        (pk, shard.at[0], lambda ref: ref.at[aligned(c * 2, 2)]),
        (pv, shard.at[1], lambda ref: ref.at[aligned(c * 2, 2)]),
        (rk, ks, lambda ref: ref.at[PBLOCKS + p * 2 + c]),
        (rv, vs, lambda ref: ref.at[PBLOCKS + p * 2 + c]),
    )
    qg_parts = [(i, h) for i in range(2) for h in range(HEADS)]
    own = []
    for i, (src, dst, part) in enumerate(kv_parts):
        own.append(pltpu.make_async_copy(src.at[:, :, aligned(c * D, D)], part(dst), own_sem.at[i]))
    for i, h in qg_parts:
        src, dst = ((q, qh), (g, gh))[i]
        own.append(
            pltpu.make_async_copy(
                src.at[:, aligned(c * 896 + h * D, D)],
                dst.at[h, aligned(c * 128, 128), :],
                qg_own.at[i * HEADS + h],
            )
        )
    for copy in own:
        copy.start()
    dkr[...] = jnp.zeros_like(dkr)
    dvr[...] = jnp.zeros_like(dvr)
    dqt[...] = jnp.zeros_like(dqt)
    ms[...] = jnp.full_like(ms, -1e30)
    ls[...] = jnp.zeros_like(ls)
    ds[...] = jnp.zeros_like(ds)
    for copy in own:
        copy.wait()

    def half_ready(half):
        rows = aligned(half * 128, 128)
        keep = lax.broadcasted_iota(jnp.int32, (128, D), 0) + (p * 256 + half * 128) < length[0]
        for h in range(HEADS):
            part = jnp.where(keep, gh[h, rows, :].astype(f32), 0.0).astype(bf16)
            gh[h, rows, :] = part
            gt[h, :, rows] = part.T
            qt[h, :, rows] = qh[h, rows, :].T

    half_ready(c)
    pl.semaphore_wait(sem, 46)
    sent = {}

    def send(key, parts):
        copy = Remote(parts)
        copy.start()
        sent[key] = copy
        return copy

    maybe_sent = {}

    def send_if(key, condition, parts):
        copy = Remote(parts)
        pl.when(condition())(copy.start)
        maybe_sent[key] = (condition, copy)
        return copy

    def drain(pending):
        for copy in pending:
            copy.wait_recv()

    def drain_if(pending):
        for condition, copy in pending:
            pl.when(condition())(copy.wait_recv)

    swaps, qg_swaps = [], []
    for i, (src, dst, part) in enumerate(kv_parts):

        def parts(i=i, src=src, dst=dst, part=part):
            return src.at[:, :, aligned((1 - c) * D, D)], part(dst), sib, sib_s.at[i], sib_r.at[i]

        swaps.append(send(("kv", i), parts))
    for i, h in qg_parts:

        def parts(i=i, h=h):
            src, dst = ((q, qh), (g, gh))[i]
            k = i * HEADS + h
            col = aligned((1 - c) * 896 + h * D, D)
            return src.at[:, col], dst.at[h, aligned(c * 128, 128), :], sib, qg_s.at[k], qg_r.at[k]

        qg_swaps.append(send(("qg", i, h), parts))
    for copy in swaps:
        copy.wait_recv()
    kv[:, p, x] = shard[:, x]

    def zy_peer(o):
        return lax.rem(z + o // 2, 8), lax.rem(y + lax.rem(o, 2), 2)

    def piece_copy(o):
        zz, yl = zy_peer(o)
        return pltpu.make_async_remote_copy(
            src_ref=shard.at[:, x],
            dst_ref=kv.at[:, p, x],
            send_sem=pz_s.at[o],
            recv_sem=pz_r.at[o],
            device_id=(r, zz * 4 + yl * 2 + c),
            device_id_type=MESH,
        )

    streams = {"v": (0, vs, y), "k": (1, ks, y), "kb": (2, ks, 1 - y)}
    pend = {}

    def block(t, line):
        return PBLOCKS + (t * 2 + line) * 2

    def passes(way, step, zz):
        if way == 0:
            return (zz <= 6) & (zz - step + 1 >= 0)
        return (zz + step - 1 >= 8) | (zz + step - 1 <= 3)

    def arrives(way, step):
        return passes(way, step, mod8(z - 1) if way == 0 else mod8(z + 1))

    def push(key, condition, ref, span, to, s_sems, r_sems, k):
        def parts():
            start, size = span()
            part = ref.at[pl.ds(start, size)]
            return part, part, to, s_sems.at[k], r_sems.at[k]

        return send_if(key, condition, parts) if condition else send(key, parts)

    def start_z(name, step):
        number, ref, line = streams[name]
        out = []
        for way, to in ways:

            def span(way=way):
                t = mod8(z - step + 1) if way == 0 else mod8(z + step - 1)
                return (block(t, line) + way, 1) if step == 4 else (block(t, line), 2)

            k = number * 8 + way * 4 + step - 1
            copy = push(("z", k), lambda way=way: passes(way, step, z), ref, span, to, rz_s, rz_r, k)
            out.append((lambda way=way: arrives(way, step), copy))
        pend[name, step] = out

    def start_vy(slot):
        def span():
            return block(mod8(z - slot), y), 2

        def seen():
            return z >= slot

        pend["vy", slot] = [(seen, push(("vy", slot), seen, vs, span, yn, vy_s, vy_r, slot))]

    def ring(step, names=("v", "k", "kb")):
        for name in names:
            drain_if(pend[name, step - 1])
            if step < 5:
                start_z(name, step)
            if name == "v":
                start_vy(step - 1)
                if step < 5:
                    start_vy(9 - step)

    pend["ky"] = [push(("ky",), None, ks, lambda: (block(z, y), 2), yn, ky_s, ky_r, 0)]
    start_z("v", 1)
    start_z("k", 1)
    start_vy(0)

    @pl.loop(1, 16)
    def _(o):
        piece_copy(o).start()

    drain(pend["ky"])
    start_z("kb", 1)
    for copy in qg_swaps:
        copy.wait_recv()
    half_ready(1 - c)
    drain_if(pend["vy", 0])
    middle = jnp.mean(vs[aligned(PBLOCKS + z * 4, 4)].reshape(KC, D).astype(f32), axis=0, keepdims=True)
    middle = jnp.broadcast_to(middle, (16, D)).astype(bf16)
    for h in range(HEADS):
        cen[h] = dot(middle, gt[h])[0:1]

    def stats(i, masked):
        rows = aligned(i * KC, KC)
        kc = ks[aligned(i * 4, 4)].reshape(KC, D)
        vc = vs[aligned(i * 4, 4)].reshape(KC, D)

        def logits(h):
            s = dot(kc, qt[h])
            if masked:
                key = lax.broadcasted_iota(jnp.int32, s.shape, 0)
                pos = lax.broadcasted_iota(jnp.int32, s.shape, 1) + y * 256
                s = jnp.where(key <= pos, s, -jnp.inf)
            sb[h % 2] = s
            return jnp.maximum(ms[h], jnp.max(s, axis=0, keepdims=True) * (SCALE * LOG2E))

        top = logits(0)
        for h in range(HEADS):
            ahead = logits(h + 1) if h + 1 < HEADS else None
            dp = dot(vc, gt[h]) - cen[h]
            back = jnp.exp2(ms[h] - top)
            w = jnp.exp2(sb[h % 2] * (SCALE * LOG2E) - top)
            ls[h] = ls[h] * back + jnp.sum(w, axis=0, keepdims=True)
            ds[h] = ds[h] * back + jnp.sum(w * dp, axis=0, keepdims=True)
            pb[h, rows, :] = w.astype(bf16)
            db[h, rows, :] = dp.astype(bf16)
            mb[i, h] = top
            ms[h] = top
            top = ahead

    stats(4 + z, True)

    def vy_ready(*slots):
        for slot in slots:
            drain_if(pend["vy", slot])

    ring(2, ("v", "k"))

    @pl.loop(1, 16)
    def _(o):
        piece_copy(o).wait()

    for half in range(2):
        pend["px", half] = []
        for dx in range(1, 4):

            def parts(half=half, dx=dx):
                k = half * 3 + dx - 1
                part = kv.at[:, pl.ds(half * 8, 8), x]
                return part, part, (lax.rem(x + dx, 4) * 2 + y_hi, b), px_s.at[k], px_r.at[k]

            pend["px", half].append(send(("px", half, dx), parts))

    ring(2, ("kb",))
    stats_events = {
        0: (lambda: vy_ready(1, 7),),
        2: (lambda: ring(3), lambda: drain(pend["px", 0])),
        4: (lambda: vy_ready(2, 6),),
        6: (lambda: ring(4), lambda: drain(pend["px", 1])),
        8: (lambda: ring(5), lambda: vy_ready(3, 5)),
        10: (lambda: vy_ready(4),),
    }
    prompt_at = {2: 0, 3: 1, 6: 2, 7: 3}
    back_at = {0: 1, 1: 7, 4: 2, 5: 6, 8: 3, 9: 5, 10: 4}

    def lookup(table, n, other):
        value = other
        for k, v in table.items():
            value = jnp.where(n == k, v, value)
        return value

    def play(events, n):
        for k, acts in events.items():

            @pl.when(n == k)
            def _():
                for act in acts:
                    act()

    @pl.loop(0, 11)
    def _(n):
        play(stats_events, n)
        chunk = lookup(prompt_at, n, 4 + z - lookup(back_at, n, 0))

        @pl.when((chunk >= 4) | (lookup(prompt_at, n, -1) >= 0))
        def _():
            stats(chunk, False)

    for h in range(HEADS):
        inv = 1.0 / ls[h]
        ls[h] = inv
        ds[h] = ds[h] * inv

    def grads(i):
        rows = aligned(i * KC, KC)
        kt = ks[aligned(i * 4, 4)].reshape(KC, D).T
        dk = jnp.zeros((KC, D), f32)
        dv = jnp.zeros((KC, D), f32)
        for h in range(HEADS):
            w = pb[h, rows, :].astype(f32) * (jnp.exp2(mb[i, h] - ms[h]) * ls[h])
            d_logit = (w * (db[h, rows, :].astype(f32) - ds[h])).astype(bf16)
            sd[h] = d_logit
            dk = dk + dot(d_logit, qh[h])
            dv = dv + dot(w.astype(bf16), gh[h])
        for h in range(HEADS):
            dqt[h] += dot(kt, sd[h])
        return (dk * SCALE).astype(bf16), dv.astype(bf16)

    kz, vz, vy = {}, {}, {}
    xc = []

    def target(way, far):
        return mod8(z + far) if way == 0 else mod8(z - far)

    def sends(way, step, zz):
        ahead = zz + 5 - step
        return (ahead >= 8) | (ahead <= 3) if way == 0 else zz >= 5 - step

    def receives(way, step):
        return sends(way, step, mod8(z - 1) if way == 0 else mod8(z + 1))

    def sees(slot):
        return mod8(z + slot) <= z

    def send_vy(slot):
        def parts():
            return dvr.at[mod8(z + slot), 1 - y], v_y.at[slot], yn, rvy_s.at[slot], rvy_r.at[slot]

        vy[slot] = send_if(("rvy", slot), lambda: sees(slot), parts)

    def wait_vy(slot, ref_index):
        @pl.when(sees(slot))
        def _():
            vy[slot].wait_recv()
            add(dvr, ref_index, v_y[slot])

    def x_send(half):
        for dx in range(1, 4):

            def parts(dx=dx):
                k = half * 3 + dx - 1
                span = pl.ds(half * 8, 8)
                xx = lax.rem(x + dx, 4)
                return dp_kv.at[:, span, xx], x_in.at[dx - 1, :, span], (xx * 2 + y_hi, b), x_s.at[k], x_r.at[k]

            xc.append(send(("x", half, dx), parts))

    def add(ref, index, *terms):
        total = ref[index].astype(f32)
        for term in terms:
            total = total + term.astype(f32)
        ref[index] = total.astype(bf16)

    k_lines = (1 - y, y)

    def k_step(step):
        for stream, line in enumerate(k_lines):
            for way, to in ways:
                t = target(way, 5 - step)
                half = pl.ds(way * 128, 128)

                def parts(stream=stream, line=line, way=way, to=to, half=half):
                    t = target(way, 5 - step)
                    k = stream * 8 + way * 4 + step - 1
                    src, dst = dkr.at[t, line], k_in.at[stream, way, step - 1]
                    if step == 1:
                        src, dst = dkr.at[t, line, half], k_in.at[stream, way, 0, half]
                    return src, dst, to, rkz_s.at[k], rkz_r.at[k]

                if step > 1:

                    @pl.when(receives(way, step - 1))
                    def _():
                        kz[stream, way, step - 1].wait_recv()
                        if step == 2:
                            add(dkr, (t, line, half), k_in[stream, way, 0, half])
                        else:
                            add(dkr, (t, line), k_in[stream, way, step - 2])

                kz[stream, way, step] = send_if(
                    ("rkz", stream, way, step), lambda way=way: sends(way, step, z), parts
                )

    def v_step(step):
        far = 5 - step
        if step == 1:
            wait_vy(4, (mod8(z + 4), y))
        for way, to in ways:
            t = target(way, far)
            half = pl.ds(way * 128, 128)

            def parts(way=way, to=to, half=half):
                t = target(way, far)
                k = way * 4 + step - 1
                src, dst = dvr.at[t, y], v_in.at[way, step - 1]
                if step == 1:
                    src, dst = dvr.at[t, y, half], v_in.at[way, 0, half]
                return src, dst, to, rvz_s.at[k], rvz_r.at[k]

            if step > 1:
                wait_vy(far if way == 0 else 8 - far, (t, y))

                @pl.when(receives(way, step - 1))
                def _():
                    vz[way, step - 1].wait_recv()
                    if step == 2:
                        add(dvr, (t, y, half), v_in[way, 0, half])
                    else:
                        add(dvr, (t, y), v_in[way, step - 2])

            vz[way, step] = send_if(("rvz", way, step), lambda way=way: sends(way, step, z), parts)

    def yz_copy(o):
        yh, zz, yl = yz_peer(o)
        return pltpu.make_async_remote_copy(
            src_ref=xs.at[:, zz * 2 + yl, aligned(yh * 16, 16), :],
            dst_ref=yz_in.at[o],
            send_sem=yz_s.at[o],
            recv_sem=yz_r.at[o],
            device_id=(x * 2 + yh, zz * 4 + yl * 2 + c),
            device_id_type=MESH,
        )

    def yz_send():
        for copy in xc:
            copy.wait_recv()
        for i in range(2):
            xs[i] = (
                dp_kv[i, :, x].astype(f32) + x_in[0, i].astype(f32) + x_in[1, i].astype(f32) + x_in[2, i].astype(f32)
            ).astype(bf16)

        @pl.loop(1, 32)
        def _(o):
            yz_copy(o).start()

    def both(far):
        send_vy(far)
        send_vy(8 - far)

    grads_events = {
        1: (lambda: k_step(1), lambda: send_vy(4)),
        3: (lambda: x_send(0),),
        4: (lambda: v_step(1),),
        5: (lambda: both(3), lambda: k_step(2)),
        7: (lambda: x_send(1),),
        8: (lambda: v_step(2),),
        9: (lambda: both(2), lambda: k_step(3)),
        11: (lambda: both(1), lambda: v_step(3)),
    }
    ahead_at = {0: 4, 3: 3, 4: 5, 7: 2, 8: 6, 9: 1, 10: 7, 11: 0}
    prompt_now = {1: 0, 2: 1, 5: 2, 6: 3}

    @pl.loop(0, 12)
    def _(n):
        play(grads_events, n)
        t = mod8(z + lookup(ahead_at, n, 0))
        is_prompt = lookup(prompt_now, n, -1) >= 0

        @pl.when(is_prompt | (t <= z))
        def _():
            chunk = lookup(prompt_now, n, 4 + t)
            dk, dv = grads(chunk)

            @pl.when(is_prompt)
            def _():
                dp_kv[0, pl.ds(chunk * 4, 4)] = dk.reshape(4, 4, 32, D)
                dp_kv[1, pl.ds(chunk * 4, 4)] = dv.reshape(4, 4, 32, D)

            @pl.when(jnp.logical_not(is_prompt))
            def _():
                dkr[t] = dk.reshape(2, 256, D)
                dvr[t] = dv.reshape(2, 256, D)

    send_vy(0)

    dq_copies = []
    for h in range(HEADS):
        dqs[h] = (dqt[h].T * SCALE).astype(bf16)
        to = gq.at[:, aligned(c * 896 + h * D, D)]
        mine = pltpu.make_async_copy(dqs.at[h, aligned(c * 128, 128), :], to, dq_own.at[h])
        mine.start()
        theirs = send(
            ("dq", h),
            lambda h=h, to=to: (dqs.at[h, aligned((1 - c) * 128, 128), :], to, sib, dq_s.at[h], dq_r.at[h]),
        )
        dq_copies.append((mine, theirs))
    yz_send()
    k_step(4)
    v_step(4)

    def last_terms(copies, ref, index, ins):
        for way in (0, 1):

            @pl.when(receives(way, 4))
            def _():
                copies(way).wait_recv()
                add(ref, index, ins(way))

    last_terms(lambda way: kz[0, way, 4], dkr, (z, 1 - y), lambda way: k_in[0, way, 3])
    ky_out[...] = dkr[z, 1 - y]
    ky = send(("rky",), lambda: (ky_out, ky_in, yn, rky_s, rky_r))

    yz_in[0] = xs[:, p, aligned(y_hi * 16, 16), :]

    @pl.loop(1, 32)
    def _(o):
        yz_copy(o).wait()

    g_out[...] = jnp.sum(yz_in[...].astype(f32), axis=0).astype(bf16)
    core = r // 4
    part = lax.rem(r, 4)
    for o in range(8):
        dst = pgkv.at[:, aligned(part * 16, 16), aligned(c * 128, 128)]
        s_sem, r_sem = g_s.at[o], g_r.at[part * 2 + c]
        to = (lax.rem(r + o, 8), p * 2 + core)
        if o == 0:

            @pl.when(core == c)
            def _():
                pltpu.make_async_copy(g_out, dst, r_sem).start()

            @pl.when(core != c)
            def _():
                pltpu.make_async_remote_copy(
                    src_ref=g_out, dst_ref=dst, send_sem=s_sem, recv_sem=r_sem, device_id=to, device_id_type=MESH
                ).start()
        else:
            send(("g", o), lambda a=(g_out, dst, to, s_sem, r_sem): a)

    last = []

    def finish(i, out):
        to = out.at[:, aligned(c * 128, 128)]
        mine = pltpu.make_async_copy(fin.at[i, aligned(c * 128, 128), :], to, f_sem.at[i])
        mine.start()
        theirs = send(
            ("fin", i),
            lambda: (fin.at[i, aligned((1 - c) * 128, 128), :], to, sib, f_sem.at[2 + i], f_sem.at[4 + i]),
        )
        last.append((mine, theirs))

    wait_vy(0, (z, y))
    last_terms(lambda way: vz[way, 4], dvr, (z, y), lambda way: v_in[way, 3])
    fin[1] = dvr[z, y]
    finish(1, gkv.at[1])
    last_terms(lambda way: kz[1, way, 4], dkr, (z, y), lambda way: k_in[1, way, 3])
    ky.wait_recv()
    fin[0] = (dkr[z, y].astype(f32) + ky_in[...].astype(f32)).astype(bf16)
    finish(0, gkv.at[0])
    for mine, theirs in last + dq_copies:
        mine.wait()
        theirs.wait_recv()
    for k in range(8):
        pltpu.make_async_copy(g_out, pgkv.at[:, 0:16, 0:128], g_r.at[k]).wait()

    @pl.when(core != c)
    def _():
        pltpu.make_async_copy(g_out, pgkv.at[:, 0:16, 0:128], g_s.at[0]).wait()

    for copy in sent.values():
        copy.wait_send()
    for condition, copy in maybe_sent.values():
        pl.when(condition())(copy.wait_send)


def hand_on_kernel(gq, gkv, pgkv, out_q, out_k, out_v, out_pk, out_pv, *held_and_sems):
    held, sems = held_and_sems[:5], held_and_sems[5]
    ins = (gq, gkv.at[0], gkv.at[1], pgkv.at[0], pgkv.at[1])
    outs = (out_q, out_k, out_v, out_pk, out_pv)
    loads = [pltpu.make_async_copy(ins[i], held[i], sems.at[i]) for i in range(5)]
    stores = [pltpu.make_async_copy(held[i], outs[i], sems.at[5 + i]) for i in range(5)]
    for copy in loads:
        copy.start()
    for load, store in zip(loads, stores):
        load.wait()
        store.start()
    for copy in stores:
        copy.wait()


def shards(q, rk, rv, pk, pv, go, lengths):
    rows = q.shape[1]
    dma = pltpu.SemaphoreType.DMA
    n_keys = PROMPT + RESP

    def out(*shape):
        return jax.ShapeDtypeStruct(shape, bf16)

    def v(*shape, dtype=bf16):
        return pltpu.VMEM(shape, dtype)

    def w(*shape):
        return pltpu.VMEM(shape, f32)

    outs = pl.pallas_call(
        fused_kernel,
        out_shape=(out(rows, 1792), out(2, rows, 256), out(2, 64, 256)),
        in_specs=[SMEM] + [ANY] * 6,
        out_specs=(ANY,) * 3,
        scratch_shapes=[
            v(HEADS, 256, D), v(HEADS, 256, D), v(HEADS, D, 256), v(HEADS, D, 256),
            v(2, n_keys // 128, 4, 32, D), v(2, 4, 32, D),
            v(HEADS, n_keys, 256), v(HEADS, n_keys, 256), w(n_keys // KC, HEADS, 1, 256),
            w(HEADS, 1, 256), w(HEADS, 1, 256), w(HEADS, 1, 256), w(HEADS, 1, 256),
            w(2, KC, 256), v(HEADS, KC, 256), w(HEADS, D, 256), v(HEADS, 256, D),
            v(8, 2, 256, D), v(8, 2, 256, D), v(2, 16, 4, 32, D),
            v(2, 2, 4, 256, D), v(2, 4, 256, D), v(8, 256, D), v(256, D), v(256, D), v(2, 256, D),
            v(3, 2, 16, 32, D), v(2, 16, 32, D), v(32, 2, 16, D), v(2, 16, D),
            dma((4,)), dma((4,)), dma((4,)), dma((14,)), dma((14,)), dma((14,)),
            dma((1,)), dma((1,)), dma((24,)), dma((24,)), dma((8,)), dma((8,)),
            dma((16,)), dma((16,)), dma((6,)), dma((6,)),
            dma((16,)), dma((16,)), dma((8,)), dma((8,)), dma((8,)), dma((8,)), dma, dma, dma((6,)),
            dma((6,)), dma((6,)), dma((32,)), dma((32,)), dma((8,)), dma((8,)), dma((7,)), dma((7,)), dma((7,)),
        ],
        compiler_params=pltpu.CompilerParams(
            collective_id=0, has_side_effects=True, vmem_limit_bytes=63 * 2**20
        ),
        name="fused",
    )(
        lengths, q[0], go[0], rk[0].reshape(4, 32, 256), rv[0].reshape(4, 32, 256),
        pk.reshape(2, 32, 256), pv.reshape(2, 32, 256),
    )
    results = ((rows, 1792), (rows, 256), (rows, 256), (64, 256), (64, 256))
    gq, gk, gv, pkg, pvg = pl.pallas_call(
        hand_on_kernel,
        out_shape=tuple(out(*shape) for shape in results),
        in_specs=[ANY] * 3,
        out_specs=(ANY,) * 5,
        scratch_shapes=[v(*shape) for shape in results] + [dma((10,))],
        compiler_params=pltpu.CompilerParams(vmem_limit_bytes=63 * 2**20),
        name="hand_on",
    )(*outs)
    return gq[None], gk[None], gv[None], pkg, pvg


def solution(mesh):
    in_specs = (
        P("resp", "blk", None),
        P("resp", "blk", None),
        P("resp", "blk", None),
        P("blk", None),
        P("blk", None),
        P("resp", "blk", None),
        P("resp"),
    )
    out_specs = (
        P("resp", "blk", None),
        P("resp", "blk", None),
        P("resp", "blk", None),
        P("blk", None),
        P("blk", None),
    )
    return jax.shard_map(shards, mesh=mesh, in_specs=in_specs, out_specs=out_specs, check_vma=False)
```

```python
import functools

import jax
import jax.numpy as jnp
from jax import lax
from jax.experimental import pallas as pl
from jax.experimental.pallas import tpu as pltpu
from jax.sharding import PartitionSpec as P

HEADS = 7
D = 128
RESP = 4096
PROMPT = 2048
PBLOCKS = PROMPT // 128
SCALE = D**-0.5
LOG2E = 1.4426950408889634
KC = 512
f32, bf16 = jnp.float32, jnp.bfloat16
MESH = pl.DeviceIdType.MESH
ANY = pl.BlockSpec(memory_space=pl.ANY)
VMEM = pl.BlockSpec(memory_space=pltpu.VMEM)
SMEM = pl.BlockSpec(memory_space=pltpu.SMEM)


def dot(a, b):
    return jnp.dot(a, b, preferred_element_type=f32)


def place():
    r, b = lax.axis_index("resp"), lax.axis_index("blk")
    z, y, c = b // 4, lax.rem(b // 2, 2), lax.rem(b, 2)
    return r, b, z, y, c


def aligned(start, size):
    return pl.ds(pl.multiple_of(start, size), size)


def mod8(value):
    return lax.rem(value + 16, 8)


class Remote:
    def __init__(self, parts):
        self.parts = parts

    def make(self):
        src, dst, to, s_sem, r_sem = self.parts()
        return pltpu.make_async_remote_copy(
            src_ref=src, dst_ref=dst, send_sem=s_sem, recv_sem=r_sem, device_id=to, device_id_type=MESH
        )

    def start(self):
        self.make().start()

    def wait_recv(self):
        self.make().wait_recv()

    def wait_send(self):
        self.make().wait_send()


def fused_kernel(
    length, q, g, rk, rv, pk, pv, gq, gkv, pgkv,
    qh, gh, qt, gt, kv, shard, pb, db, mb, ms, ls, ds, cen, sb, sd, dqt, dqs,
    dkr, dvr, dp_kv, k_in, v_in, v_y, ky_out, ky_in, fin, x_in, xs, yz_in, g_out,
    own_sem, sib_s, sib_r, qg_own, qg_s, qg_r,
    ky_s, ky_r, rz_s, rz_r, vy_s, vy_r, pz_s, pz_r, px_s, px_r,
    rkz_s, rkz_r, rvz_s, rvz_r, rvy_s, rvy_r, rky_s, rky_r, f_sem,
    x_s, x_r, yz_s, yz_r, g_s, g_r, dq_own, dq_s, dq_r,
):
    r, b, z, y, c = place()
    x, y_hi = r // 2, lax.rem(r, 2)
    p = z * 2 + y
    ks, vs = kv.at[0], kv.at[1]
    sib = (r, b + 1 - 2 * c)
    yn = (r, b + 2 - 4 * y)
    zr = (r, lax.rem(b + 4, 32))
    zl = (r, lax.rem(b + 28, 32))
    ways = ((0, zr), (1, zl))

    def yz_peer(o):
        yh = lax.rem(y_hi + o // 16, 2)
        zz = lax.rem(z + lax.rem(o // 2, 8), 8)
        yl = lax.rem(y + lax.rem(o, 2), 2)
        return yh, zz, yl

    sem = pltpu.get_barrier_semaphore()

    @pl.loop(1, 32)
    def _(o):
        yh, zz, yl = yz_peer(o)
        pl.semaphore_signal(sem, inc=1, device_id=(x * 2 + yh, zz * 4 + yl * 2 + c), device_id_type=MESH)

    @pl.loop(1, 16)
    def _(o):
        rr = lax.rem(r + o // 2, 8)
        cc = lax.rem(c + lax.rem(o, 2), 2)
        pl.semaphore_signal(sem, inc=1, device_id=(rr, p * 2 + cc), device_id_type=MESH)

    kv_parts = (
        (pk, shard.at[0], lambda ref: ref.at[aligned(c * 2, 2)]),
        (pv, shard.at[1], lambda ref: ref.at[aligned(c * 2, 2)]),
        (rk, ks, lambda ref: ref.at[PBLOCKS + p * 2 + c]),
        (rv, vs, lambda ref: ref.at[PBLOCKS + p * 2 + c]),
    )
    qg_parts = [(i, h) for i in range(2) for h in range(HEADS)]
    own = []
    for i, (src, dst, part) in enumerate(kv_parts):
        own.append(pltpu.make_async_copy(src.at[:, :, aligned(c * D, D)], part(dst), own_sem.at[i]))
    for i, h in qg_parts:
        src, dst = ((q, qh), (g, gh))[i]
        own.append(
            pltpu.make_async_copy(
                src.at[:, aligned(c * 896 + h * D, D)],
                dst.at[h, aligned(c * 128, 128), :],
                qg_own.at[i * HEADS + h],
            )
        )
    for copy in own:
        copy.start()
    dkr[...] = jnp.zeros_like(dkr)
    dvr[...] = jnp.zeros_like(dvr)
    dqt[...] = jnp.zeros_like(dqt)
    ms[...] = jnp.full_like(ms, -1e30)
    ls[...] = jnp.zeros_like(ls)
    ds[...] = jnp.zeros_like(ds)
    for copy in own:
        copy.wait()

    def half_ready(half):
        rows = aligned(half * 128, 128)
        keep = lax.broadcasted_iota(jnp.int32, (128, D), 0) + (p * 256 + half * 128) < length[0]
        for h in range(HEADS):
            part = jnp.where(keep, gh[h, rows, :].astype(f32), 0.0).astype(bf16)
            gh[h, rows, :] = part
            gt[h, :, rows] = part.T
            qt[h, :, rows] = qh[h, rows, :].T

    half_ready(c)
    pl.semaphore_wait(sem, 46)
    sent = {}

    def send(key, parts):
        copy = Remote(parts)
        copy.start()
        sent[key] = copy
        return copy

    maybe_sent = {}

    def send_if(key, condition, parts):
        copy = Remote(parts)
        pl.when(condition())(copy.start)
        maybe_sent[key] = (condition, copy)
        return copy

    def drain(pending):
        for copy in pending:
            copy.wait_recv()

    def drain_if(pending):
        for condition, copy in pending:
            pl.when(condition())(copy.wait_recv)

    swaps, qg_swaps = [], []
    for i, (src, dst, part) in enumerate(kv_parts):

        def parts(i=i, src=src, dst=dst, part=part):
            return src.at[:, :, aligned((1 - c) * D, D)], part(dst), sib, sib_s.at[i], sib_r.at[i]

        swaps.append(send(("kv", i), parts))
    for i, h in qg_parts:

        def parts(i=i, h=h):
            src, dst = ((q, qh), (g, gh))[i]
            k = i * HEADS + h
            col = aligned((1 - c) * 896 + h * D, D)
            return src.at[:, col], dst.at[h, aligned(c * 128, 128), :], sib, qg_s.at[k], qg_r.at[k]

        qg_swaps.append(send(("qg", i, h), parts))
    for copy in swaps:
        copy.wait_recv()
    kv[:, p, x] = shard[:, x]

    def zy_peer(o):
        return lax.rem(z + o // 2, 8), lax.rem(y + lax.rem(o, 2), 2)

    def piece_copy(o):
        zz, yl = zy_peer(o)
        return pltpu.make_async_remote_copy(
            src_ref=shard.at[:, x],
            dst_ref=kv.at[:, p, x],
            send_sem=pz_s.at[o],
            recv_sem=pz_r.at[o],
            device_id=(r, zz * 4 + yl * 2 + c),
            device_id_type=MESH,
        )

    streams = {"v": (0, vs, y), "k": (1, ks, y), "kb": (2, ks, 1 - y)}
    pend = {}

    def block(t, line):
        return PBLOCKS + (t * 2 + line) * 2

    def passes(way, step, zz):
        if way == 0:
            return (zz <= 6) & (zz - step + 1 >= 0)
        return (zz + step - 1 >= 8) | (zz + step - 1 <= 3)

    def arrives(way, step):
        return passes(way, step, mod8(z - 1) if way == 0 else mod8(z + 1))

    def push(key, condition, ref, span, to, s_sems, r_sems, k):
        def parts():
            start, size = span()
            part = ref.at[pl.ds(start, size)]
            return part, part, to, s_sems.at[k], r_sems.at[k]

        return send_if(key, condition, parts) if condition else send(key, parts)

    def start_z(name, step):
        number, ref, line = streams[name]
        out = []
        for way, to in ways:

            def span(way=way):
                t = mod8(z - step + 1) if way == 0 else mod8(z + step - 1)
                return (block(t, line) + way, 1) if step == 4 else (block(t, line), 2)

            k = number * 8 + way * 4 + step - 1
            copy = push(("z", k), lambda way=way: passes(way, step, z), ref, span, to, rz_s, rz_r, k)
            out.append((lambda way=way: arrives(way, step), copy))
        pend[name, step] = out

    def start_vy(slot):
        def span():
            return block(mod8(z - slot), y), 2

        def seen():
            return z >= slot

        pend["vy", slot] = [(seen, push(("vy", slot), seen, vs, span, yn, vy_s, vy_r, slot))]

    def ring(step, names=("v", "k", "kb")):
        for name in names:
            drain_if(pend[name, step - 1])
            if step < 5:
                start_z(name, step)
            if name == "v":
                start_vy(step - 1)
                if step < 5:
                    start_vy(9 - step)

    @pl.loop(1, 16)
    def _(o):
        piece_copy(o).start()

    pend["ky"] = [push(("ky",), None, ks, lambda: (block(z, y), 2), yn, ky_s, ky_r, 0)]
    start_z("v", 1)
    start_z("k", 1)
    start_vy(0)

    drain(pend["ky"])
    start_z("kb", 1)
    for copy in qg_swaps:
        copy.wait_recv()
    half_ready(1 - c)
    drain_if(pend["vy", 0])
    middle = jnp.mean(vs[aligned(PBLOCKS + z * 4, 4)].reshape(KC, D).astype(f32), axis=0, keepdims=True)
    middle = jnp.broadcast_to(middle, (16, D)).astype(bf16)
    for h in range(HEADS):
        cen[h] = dot(middle, gt[h])[0:1]

    def stats(i, masked):
        rows = aligned(i * KC, KC)
        kc = ks[aligned(i * 4, 4)].reshape(KC, D)
        vc = vs[aligned(i * 4, 4)].reshape(KC, D)

        def logits(h):
            s = dot(kc, qt[h])
            if masked:
                key = lax.broadcasted_iota(jnp.int32, s.shape, 0)
                pos = lax.broadcasted_iota(jnp.int32, s.shape, 1) + y * 256
                s = jnp.where(key <= pos, s, -jnp.inf)
            sb[h % 2] = s
            return jnp.maximum(ms[h], jnp.max(s, axis=0, keepdims=True) * (SCALE * LOG2E))

        top = logits(0)
        for h in range(HEADS):
            ahead = logits(h + 1) if h + 1 < HEADS else None
            dp = dot(vc, gt[h]) - cen[h]
            back = jnp.exp2(ms[h] - top)
            w = jnp.exp2(sb[h % 2] * (SCALE * LOG2E) - top)
            ls[h] = ls[h] * back + jnp.sum(w, axis=0, keepdims=True)
            ds[h] = ds[h] * back + jnp.sum(w * dp, axis=0, keepdims=True)
            pb[h, rows, :] = w.astype(bf16)
            db[h, rows, :] = dp.astype(bf16)
            mb[i, h] = top
            ms[h] = top
            top = ahead

    stats(4 + z, True)

    def vy_ready(*slots):
        for slot in slots:
            drain_if(pend["vy", slot])

    ring(2, ("v", "k"))

    @pl.loop(1, 16)
    def _(o):
        piece_copy(o).wait()

    for half in range(2):
        pend["px", half] = []
        for dx in range(1, 4):

            def parts(half=half, dx=dx):
                k = half * 3 + dx - 1
                part = kv.at[:, pl.ds(half * 8, 8), x]
                return part, part, (lax.rem(x + dx, 4) * 2 + y_hi, b), px_s.at[k], px_r.at[k]

            pend["px", half].append(send(("px", half, dx), parts))

    ring(2, ("kb",))
    stats_events = {
        0: (lambda: vy_ready(1, 7),),
        1: (lambda: ring(3),),
        2: (lambda: drain(pend["px", 0]),),
        4: (lambda: ring(4), lambda: vy_ready(2, 6)),
        6: (lambda: drain(pend["px", 1]),),
        7: (lambda: ring(5),),
        8: (lambda: vy_ready(3, 5),),
        10: (lambda: vy_ready(4),),
    }
    prompt_at = {2: 0, 3: 1, 6: 2, 7: 3}
    back_at = {0: 1, 1: 7, 4: 2, 5: 6, 8: 3, 9: 5, 10: 4}

    def lookup(table, n, other):
        value = other
        for k, v in table.items():
            value = jnp.where(n == k, v, value)
        return value

    def play(events, n):
        for k, acts in events.items():

            @pl.when(n == k)
            def _():
                for act in acts:
                    act()

    @pl.loop(0, 11)
    def _(n):
        play(stats_events, n)
        chunk = lookup(prompt_at, n, 4 + z - lookup(back_at, n, 0))

        @pl.when((chunk >= 4) | (lookup(prompt_at, n, -1) >= 0))
        def _():
            stats(chunk, False)

    for h in range(HEADS):
        inv = 1.0 / ls[h]
        ls[h] = inv
        ds[h] = ds[h] * inv

    def grads(i):
        rows = aligned(i * KC, KC)
        kt = ks[aligned(i * 4, 4)].reshape(KC, D).T
        dk = jnp.zeros((KC, D), f32)
        dv = jnp.zeros((KC, D), f32)
        for h in range(HEADS):
            w = pb[h, rows, :].astype(f32) * (jnp.exp2(mb[i, h] - ms[h]) * ls[h])
            d_logit = (w * (db[h, rows, :].astype(f32) - ds[h])).astype(bf16)
            sd[h] = d_logit
            dk = dk + dot(d_logit, qh[h])
            dv = dv + dot(w.astype(bf16), gh[h])
        for h in range(HEADS):
            dqt[h] += dot(kt, sd[h])
        return (dk * SCALE).astype(bf16), dv.astype(bf16)

    kz, vz, vy = {}, {}, {}
    xc = []

    def target(way, far):
        return mod8(z + far) if way == 0 else mod8(z - far)

    def sends(way, step, zz):
        ahead = zz + 5 - step
        return (ahead >= 8) | (ahead <= 3) if way == 0 else zz >= 5 - step

    def receives(way, step):
        return sends(way, step, mod8(z - 1) if way == 0 else mod8(z + 1))

    def sees(slot):
        return mod8(z + slot) <= z

    def send_vy(slot):
        def parts():
            return dvr.at[mod8(z + slot), 1 - y], v_y.at[slot], yn, rvy_s.at[slot], rvy_r.at[slot]

        vy[slot] = send_if(("rvy", slot), lambda: sees(slot), parts)

    def wait_vy(slot, ref_index):
        @pl.when(sees(slot))
        def _():
            vy[slot].wait_recv()
            add(dvr, ref_index, v_y[slot])

    def x_send(half):
        for dx in range(1, 4):

            def parts(dx=dx):
                k = half * 3 + dx - 1
                span = pl.ds(half * 8, 8)
                xx = lax.rem(x + dx, 4)
                return dp_kv.at[:, span, xx], x_in.at[dx - 1, :, span], (xx * 2 + y_hi, b), x_s.at[k], x_r.at[k]

            xc.append(send(("x", half, dx), parts))

    def add(ref, index, *terms):
        total = ref[index].astype(f32)
        for term in terms:
            total = total + term.astype(f32)
        ref[index] = total.astype(bf16)

    k_lines = (1 - y, y)

    def k_step(step):
        for stream, line in enumerate(k_lines):
            for way, to in ways:
                t = target(way, 5 - step)
                half = pl.ds(way * 128, 128)

                def parts(stream=stream, line=line, way=way, to=to, half=half):
                    t = target(way, 5 - step)
                    k = stream * 8 + way * 4 + step - 1
                    src, dst = dkr.at[t, line], k_in.at[stream, way, step - 1]
                    if step == 1:
                        src, dst = dkr.at[t, line, half], k_in.at[stream, way, 0, half]
                    return src, dst, to, rkz_s.at[k], rkz_r.at[k]

                if step > 1:

                    @pl.when(receives(way, step - 1))
                    def _():
                        kz[stream, way, step - 1].wait_recv()
                        if step == 2:
                            add(dkr, (t, line, half), k_in[stream, way, 0, half])
                        else:
                            add(dkr, (t, line), k_in[stream, way, step - 2])

                kz[stream, way, step] = send_if(
                    ("rkz", stream, way, step), lambda way=way: sends(way, step, z), parts
                )

    def v_step(step):
        far = 5 - step
        if step == 1:
            wait_vy(4, (mod8(z + 4), y))
        for way, to in ways:
            t = target(way, far)
            half = pl.ds(way * 128, 128)

            def parts(way=way, to=to, half=half):
                t = target(way, far)
                k = way * 4 + step - 1
                src, dst = dvr.at[t, y], v_in.at[way, step - 1]
                if step == 1:
                    src, dst = dvr.at[t, y, half], v_in.at[way, 0, half]
                return src, dst, to, rvz_s.at[k], rvz_r.at[k]

            if step > 1:
                wait_vy(far if way == 0 else 8 - far, (t, y))

                @pl.when(receives(way, step - 1))
                def _():
                    vz[way, step - 1].wait_recv()
                    if step == 2:
                        add(dvr, (t, y, half), v_in[way, 0, half])
                    else:
                        add(dvr, (t, y), v_in[way, step - 2])

            vz[way, step] = send_if(("rvz", way, step), lambda way=way: sends(way, step, z), parts)

    def yz_copy(o):
        yh, zz, yl = yz_peer(o)
        return pltpu.make_async_remote_copy(
            src_ref=xs.at[:, zz * 2 + yl, aligned(yh * 16, 16), :],
            dst_ref=yz_in.at[o],
            send_sem=yz_s.at[o],
            recv_sem=yz_r.at[o],
            device_id=(x * 2 + yh, zz * 4 + yl * 2 + c),
            device_id_type=MESH,
        )

    def yz_send():
        for copy in xc:
            copy.wait_recv()
        for i in range(2):
            xs[i] = (
                dp_kv[i, :, x].astype(f32) + x_in[0, i].astype(f32) + x_in[1, i].astype(f32) + x_in[2, i].astype(f32)
            ).astype(bf16)

        @pl.loop(1, 32)
        def _(o):
            yz_copy(o).start()

    def both(far):
        send_vy(far)
        send_vy(8 - far)

    grads_events = {
        1: (lambda: k_step(1), lambda: send_vy(4)),
        3: (lambda: x_send(0),),
        4: (lambda: v_step(1),),
        5: (lambda: both(3), lambda: k_step(2)),
        7: (lambda: x_send(1),),
        8: (lambda: v_step(2),),
        9: (lambda: both(2), lambda: k_step(3)),
        11: (lambda: both(1), lambda: v_step(3)),
    }
    ahead_at = {0: 4, 3: 3, 4: 5, 7: 2, 8: 6, 9: 1, 10: 7, 11: 0}
    prompt_now = {1: 0, 2: 1, 5: 2, 6: 3}

    @pl.loop(0, 12)
    def _(n):
        play(grads_events, n)
        t = mod8(z + lookup(ahead_at, n, 0))
        is_prompt = lookup(prompt_now, n, -1) >= 0

        @pl.when(is_prompt | (t <= z))
        def _():
            chunk = lookup(prompt_now, n, 4 + t)
            dk, dv = grads(chunk)

            @pl.when(is_prompt)
            def _():
                dp_kv[0, pl.ds(chunk * 4, 4)] = dk.reshape(4, 4, 32, D)
                dp_kv[1, pl.ds(chunk * 4, 4)] = dv.reshape(4, 4, 32, D)

            @pl.when(jnp.logical_not(is_prompt))
            def _():
                dkr[t] = dk.reshape(2, 256, D)
                dvr[t] = dv.reshape(2, 256, D)

    send_vy(0)

    yz_send()
    k_step(4)
    v_step(4)

    dq_copies = []
    for h in range(HEADS):
        dqs[h] = (dqt[h].T * SCALE).astype(bf16)
        to = gq.at[:, aligned(c * 896 + h * D, D)]
        mine = pltpu.make_async_copy(dqs.at[h, aligned(c * 128, 128), :], to, dq_own.at[h])
        mine.start()
        theirs = send(
            ("dq", h),
            lambda h=h, to=to: (dqs.at[h, aligned((1 - c) * 128, 128), :], to, sib, dq_s.at[h], dq_r.at[h]),
        )
        dq_copies.append((mine, theirs))

    yz_in[0] = xs[:, p, aligned(y_hi * 16, 16), :]

    @pl.loop(1, 32)
    def _(o):
        yz_copy(o).wait()

    g_out[...] = jnp.sum(yz_in[...].astype(f32), axis=0).astype(bf16)
    core = r // 4
    part = lax.rem(r, 4)
    for o in range(8):
        dst = pgkv.at[:, aligned(part * 16, 16), aligned(c * 128, 128)]
        s_sem, r_sem = g_s.at[o], g_r.at[part * 2 + c]
        to = (lax.rem(r + o, 8), p * 2 + core)
        if o == 0:

            @pl.when(core == c)
            def _():
                pltpu.make_async_copy(g_out, dst, r_sem).start()

            @pl.when(core != c)
            def _():
                pltpu.make_async_remote_copy(
                    src_ref=g_out, dst_ref=dst, send_sem=s_sem, recv_sem=r_sem, device_id=to, device_id_type=MESH
                ).start()
        else:
            send(("g", o), lambda a=(g_out, dst, to, s_sem, r_sem): a)

    def last_terms(copies, ref, index, ins):
        for way in (0, 1):

            @pl.when(receives(way, 4))
            def _():
                copies(way).wait_recv()
                add(ref, index, ins(way))

    last_terms(lambda way: kz[0, way, 4], dkr, (z, 1 - y), lambda way: k_in[0, way, 3])
    ky_out[...] = dkr[z, 1 - y]
    ky = send(("rky",), lambda: (ky_out, ky_in, yn, rky_s, rky_r))

    last = []

    def finish(i, out):
        to = out.at[:, aligned(c * 128, 128)]
        mine = pltpu.make_async_copy(fin.at[i, aligned(c * 128, 128), :], to, f_sem.at[i])
        mine.start()
        theirs = send(
            ("fin", i),
            lambda: (fin.at[i, aligned((1 - c) * 128, 128), :], to, sib, f_sem.at[2 + i], f_sem.at[4 + i]),
        )
        last.append((mine, theirs))

    wait_vy(0, (z, y))
    last_terms(lambda way: vz[way, 4], dvr, (z, y), lambda way: v_in[way, 3])
    fin[1] = dvr[z, y]
    finish(1, gkv.at[1])
    last_terms(lambda way: kz[1, way, 4], dkr, (z, y), lambda way: k_in[1, way, 3])
    ky.wait_recv()
    fin[0] = (dkr[z, y].astype(f32) + ky_in[...].astype(f32)).astype(bf16)
    finish(0, gkv.at[0])
    for mine, theirs in last + dq_copies:
        mine.wait()
        theirs.wait_recv()
    for k in range(8):
        pltpu.make_async_copy(g_out, pgkv.at[:, 0:16, 0:128], g_r.at[k]).wait()

    @pl.when(core != c)
    def _():
        pltpu.make_async_copy(g_out, pgkv.at[:, 0:16, 0:128], g_s.at[0]).wait()

    for copy in sent.values():
        copy.wait_send()
    for condition, copy in maybe_sent.values():
        pl.when(condition())(copy.wait_send)


def hand_on_kernel(gq, gkv, pgkv, out_q, out_k, out_v, out_pk, out_pv, *held_and_sems):
    held, sems = held_and_sems[:5], held_and_sems[5]
    ins = (gq, gkv.at[0], gkv.at[1], pgkv.at[0], pgkv.at[1])
    outs = (out_q, out_k, out_v, out_pk, out_pv)
    loads = [pltpu.make_async_copy(ins[i], held[i], sems.at[i]) for i in range(5)]
    stores = [pltpu.make_async_copy(held[i], outs[i], sems.at[5 + i]) for i in range(5)]
    for copy in loads:
        copy.start()
    for load, store in zip(loads, stores):
        load.wait()
        store.start()
    for copy in stores:
        copy.wait()


def shards(q, rk, rv, pk, pv, go, lengths):
    rows = q.shape[1]
    dma = pltpu.SemaphoreType.DMA
    n_keys = PROMPT + RESP

    def out(*shape):
        return jax.ShapeDtypeStruct(shape, bf16)

    def v(*shape, dtype=bf16):
        return pltpu.VMEM(shape, dtype)

    def w(*shape):
        return pltpu.VMEM(shape, f32)

    outs = pl.pallas_call(
        fused_kernel,
        out_shape=(out(rows, 1792), out(2, rows, 256), out(2, 64, 256)),
        in_specs=[SMEM] + [ANY] * 6,
        out_specs=(ANY,) * 3,
        scratch_shapes=[
            v(HEADS, 256, D), v(HEADS, 256, D), v(HEADS, D, 256), v(HEADS, D, 256),
            v(2, n_keys // 128, 4, 32, D), v(2, 4, 32, D),
            v(HEADS, n_keys, 256), v(HEADS, n_keys, 256), w(n_keys // KC, HEADS, 1, 256),
            w(HEADS, 1, 256), w(HEADS, 1, 256), w(HEADS, 1, 256), w(HEADS, 1, 256),
            w(2, KC, 256), v(HEADS, KC, 256), w(HEADS, D, 256), v(HEADS, 256, D),
            v(8, 2, 256, D), v(8, 2, 256, D), v(2, 16, 4, 32, D),
            v(2, 2, 4, 256, D), v(2, 4, 256, D), v(8, 256, D), v(256, D), v(256, D), v(2, 256, D),
            v(3, 2, 16, 32, D), v(2, 16, 32, D), v(32, 2, 16, D), v(2, 16, D),
            dma((4,)), dma((4,)), dma((4,)), dma((14,)), dma((14,)), dma((14,)),
            dma((1,)), dma((1,)), dma((24,)), dma((24,)), dma((8,)), dma((8,)),
            dma((16,)), dma((16,)), dma((6,)), dma((6,)),
            dma((16,)), dma((16,)), dma((8,)), dma((8,)), dma((8,)), dma((8,)), dma, dma, dma((6,)),
            dma((6,)), dma((6,)), dma((32,)), dma((32,)), dma((8,)), dma((8,)), dma((7,)), dma((7,)), dma((7,)),
        ],
        compiler_params=pltpu.CompilerParams(
            collective_id=0, has_side_effects=True, vmem_limit_bytes=63 * 2**20
        ),
        name="fused",
    )(
        lengths, q[0], go[0], rk[0].reshape(4, 32, 256), rv[0].reshape(4, 32, 256),
        pk.reshape(2, 32, 256), pv.reshape(2, 32, 256),
    )
    results = ((rows, 1792), (rows, 256), (rows, 256), (64, 256), (64, 256))
    gq, gk, gv, pkg, pvg = pl.pallas_call(
        hand_on_kernel,
        out_shape=tuple(out(*shape) for shape in results),
        in_specs=[ANY] * 3,
        out_specs=(ANY,) * 5,
        scratch_shapes=[v(*shape) for shape in results] + [dma((10,))],
        compiler_params=pltpu.CompilerParams(vmem_limit_bytes=63 * 2**20),
        name="hand_on",
    )(*outs)
    return gq[None], gk[None], gv[None], pkg, pvg


def solution(mesh):
    in_specs = (
        P("resp", "blk", None),
        P("resp", "blk", None),
        P("resp", "blk", None),
        P("blk", None),
        P("blk", None),
        P("resp", "blk", None),
        P("resp"),
    )
    out_specs = (
        P("resp", "blk", None),
        P("resp", "blk", None),
        P("resp", "blk", None),
        P("blk", None),
        P("blk", None),
    )
    return jax.shard_map(shards, mesh=mesh, in_specs=in_specs, out_specs=out_specs, check_vma=False)
```

```python
import functools

import jax
import jax.numpy as jnp
from jax import lax
from jax.experimental import pallas as pl
from jax.experimental.pallas import tpu as pltpu
from jax.sharding import PartitionSpec as P

HEADS = 7
D = 128
RESP = 4096
PROMPT = 2048
PBLOCKS = PROMPT // 128
SCALE = D**-0.5
LOG2E = 1.4426950408889634
KC = 512
f32, bf16 = jnp.float32, jnp.bfloat16
MESH = pl.DeviceIdType.MESH
ANY = pl.BlockSpec(memory_space=pl.ANY)
VMEM = pl.BlockSpec(memory_space=pltpu.VMEM)
SMEM = pl.BlockSpec(memory_space=pltpu.SMEM)


def dot(a, b):
    return jnp.dot(a, b, preferred_element_type=f32)


def place():
    r, b = lax.axis_index("resp"), lax.axis_index("blk")
    z, y, c = b // 4, lax.rem(b // 2, 2), lax.rem(b, 2)
    return r, b, z, y, c


def aligned(start, size):
    return pl.ds(pl.multiple_of(start, size), size)


def mod8(value):
    return lax.rem(value + 16, 8)


class Remote:
    def __init__(self, parts):
        self.parts = parts

    def make(self):
        src, dst, to, s_sem, r_sem = self.parts()
        return pltpu.make_async_remote_copy(
            src_ref=src, dst_ref=dst, send_sem=s_sem, recv_sem=r_sem, device_id=to, device_id_type=MESH
        )

    def start(self):
        self.make().start()

    def wait_recv(self):
        self.make().wait_recv()

    def wait_send(self):
        self.make().wait_send()


def fused_kernel(
    length, q, g, rk, rv, pk, pv, gq, gkv, pgkv,
    qh, gh, qt, gt, kv, shard, pb, db, mb, ms, ls, ds, cen, sb, sd, dqt, dqs,
    dkr, dvr, dp_kv, k_in, v_in, v_y, ky_out, ky_in, fin, x_in, xs, yz_in, g_out,
    own_sem, sib_s, sib_r, qg_own, qg_s, qg_r,
    ky_s, ky_r, rz_s, rz_r, vy_s, vy_r, pz_s, pz_r, px_s, px_r,
    rkz_s, rkz_r, rvz_s, rvz_r, rvy_s, rvy_r, rky_s, rky_r, f_sem,
    x_s, x_r, yz_s, yz_r, g_s, g_r, dq_own, dq_s, dq_r,
):
    r, b, z, y, c = place()
    x, y_hi = r // 2, lax.rem(r, 2)
    p = z * 2 + y
    ks, vs = kv.at[0], kv.at[1]
    sib = (r, b + 1 - 2 * c)
    yn = (r, b + 2 - 4 * y)
    zr = (r, lax.rem(b + 4, 32))
    zl = (r, lax.rem(b + 28, 32))
    ways = ((0, zr), (1, zl))

    def yz_peer(o):
        yh = lax.rem(y_hi + o // 16, 2)
        zz = lax.rem(z + lax.rem(o // 2, 8), 8)
        yl = lax.rem(y + lax.rem(o, 2), 2)
        return yh, zz, yl

    sem = pltpu.get_barrier_semaphore()

    @pl.loop(1, 32)
    def _(o):
        yh, zz, yl = yz_peer(o)
        pl.semaphore_signal(sem, inc=1, device_id=(x * 2 + yh, zz * 4 + yl * 2 + c), device_id_type=MESH)

    @pl.loop(1, 16)
    def _(o):
        rr = lax.rem(r + o // 2, 8)
        cc = lax.rem(c + lax.rem(o, 2), 2)
        pl.semaphore_signal(sem, inc=1, device_id=(rr, p * 2 + cc), device_id_type=MESH)

    kv_parts = (
        (pk, shard.at[0], lambda ref: ref.at[aligned(c * 2, 2)]),
        (pv, shard.at[1], lambda ref: ref.at[aligned(c * 2, 2)]),
        (rk, ks, lambda ref: ref.at[PBLOCKS + p * 2 + c]),
        (rv, vs, lambda ref: ref.at[PBLOCKS + p * 2 + c]),
    )
    qg_parts = [(i, h) for i in range(2) for h in range(HEADS)]
    own = []
    for i, (src, dst, part) in enumerate(kv_parts):
        own.append(pltpu.make_async_copy(src.at[:, :, aligned(c * D, D)], part(dst), own_sem.at[i]))
    for i, h in qg_parts:
        src, dst = ((q, qh), (g, gh))[i]
        own.append(
            pltpu.make_async_copy(
                src.at[:, aligned(c * 896 + h * D, D)],
                dst.at[h, aligned(c * 128, 128), :],
                qg_own.at[i * HEADS + h],
            )
        )
    for copy in own:
        copy.start()
    dkr[...] = jnp.zeros_like(dkr)
    dvr[...] = jnp.zeros_like(dvr)
    dqt[...] = jnp.zeros_like(dqt)
    ms[...] = jnp.full_like(ms, -1e30)
    ls[...] = jnp.zeros_like(ls)
    ds[...] = jnp.zeros_like(ds)
    for copy in own:
        copy.wait()

    def half_ready(half):
        rows = aligned(half * 128, 128)
        keep = lax.broadcasted_iota(jnp.int32, (128, D), 0) + (p * 256 + half * 128) < length[0]
        for h in range(HEADS):
            part = jnp.where(keep, gh[h, rows, :].astype(f32), 0.0).astype(bf16)
            gh[h, rows, :] = part
            gt[h, :, rows] = part.T
            qt[h, :, rows] = qh[h, rows, :].T

    half_ready(c)
    pl.semaphore_wait(sem, 46)
    sent = {}

    def send(key, parts):
        copy = Remote(parts)
        copy.start()
        sent[key] = copy
        return copy

    maybe_sent = {}

    def send_if(key, condition, parts):
        copy = Remote(parts)
        pl.when(condition())(copy.start)
        maybe_sent[key] = (condition, copy)
        return copy

    def drain(pending):
        for copy in pending:
            copy.wait_recv()

    def drain_if(pending):
        for condition, copy in pending:
            pl.when(condition())(copy.wait_recv)

    swaps, qg_swaps = [], []
    for i, (src, dst, part) in enumerate(kv_parts):

        def parts(i=i, src=src, dst=dst, part=part):
            return src.at[:, :, aligned((1 - c) * D, D)], part(dst), sib, sib_s.at[i], sib_r.at[i]

        swaps.append(send(("kv", i), parts))
    for i, h in qg_parts:

        def parts(i=i, h=h):
            src, dst = ((q, qh), (g, gh))[i]
            k = i * HEADS + h
            col = aligned((1 - c) * 896 + h * D, D)
            return src.at[:, col], dst.at[h, aligned(c * 128, 128), :], sib, qg_s.at[k], qg_r.at[k]

        qg_swaps.append(send(("qg", i, h), parts))
    for copy in swaps:
        copy.wait_recv()
    kv[:, p, x] = shard[:, x]

    def zy_peer(o):
        return lax.rem(z + o // 2, 8), lax.rem(y + lax.rem(o, 2), 2)

    def piece_copy(o):
        zz, yl = zy_peer(o)
        return pltpu.make_async_remote_copy(
            src_ref=shard.at[:, x],
            dst_ref=kv.at[:, p, x],
            send_sem=pz_s.at[o],
            recv_sem=pz_r.at[o],
            device_id=(r, zz * 4 + yl * 2 + c),
            device_id_type=MESH,
        )

    streams = {"v": (0, vs, y), "k": (1, ks, y), "kb": (2, ks, 1 - y)}
    pend = {}

    def block(t, line):
        return PBLOCKS + (t * 2 + line) * 2

    def passes(way, step, zz):
        if way == 0:
            return (zz <= 6) & (zz - step + 1 >= 0)
        return (zz + step - 1 >= 8) | (zz + step - 1 <= 3)

    def arrives(way, step):
        return passes(way, step, mod8(z - 1) if way == 0 else mod8(z + 1))

    def push(key, condition, ref, span, to, s_sems, r_sems, k):
        def parts():
            start, size = span()
            part = ref.at[pl.ds(start, size)]
            return part, part, to, s_sems.at[k], r_sems.at[k]

        return send_if(key, condition, parts) if condition else send(key, parts)

    def start_z(name, step):
        number, ref, line = streams[name]
        out = []
        for way, to in ways:

            def span(way=way):
                t = mod8(z - step + 1) if way == 0 else mod8(z + step - 1)
                return (block(t, line) + way, 1) if step == 4 else (block(t, line), 2)

            k = number * 8 + way * 4 + step - 1
            copy = push(("z", k), lambda way=way: passes(way, step, z), ref, span, to, rz_s, rz_r, k)
            out.append((lambda way=way: arrives(way, step), copy))
        pend[name, step] = out

    def start_vy(slot):
        def span():
            return block(mod8(z - slot), y), 2

        def seen():
            return z >= slot

        pend["vy", slot] = [(seen, push(("vy", slot), seen, vs, span, yn, vy_s, vy_r, slot))]

    def ring(step, names=("v", "k", "kb")):
        for name in names:
            drain_if(pend[name, step - 1])
            if step < 5:
                start_z(name, step)
            if name == "v":
                start_vy(step - 1)
                if step < 5:
                    start_vy(9 - step)

    @pl.loop(1, 16)
    def _(o):
        piece_copy(o).start()

    pend["ky"] = [push(("ky",), None, ks, lambda: (block(z, y), 2), yn, ky_s, ky_r, 0)]
    start_z("v", 1)
    start_z("k", 1)
    start_vy(0)

    drain(pend["ky"])
    start_z("kb", 1)
    for copy in qg_swaps:
        copy.wait_recv()
    half_ready(1 - c)
    drain_if(pend["vy", 0])
    middle = jnp.mean(vs[aligned(PBLOCKS + z * 4, 4)].reshape(KC, D).astype(f32), axis=0, keepdims=True)
    middle = jnp.broadcast_to(middle, (16, D)).astype(bf16)
    for h in range(HEADS):
        cen[h] = dot(middle, gt[h])[0:1]

    def stats(i, masked):
        rows = aligned(i * KC, KC)
        kc = ks[aligned(i * 4, 4)].reshape(KC, D)
        vc = vs[aligned(i * 4, 4)].reshape(KC, D)

        def logits(h):
            s = dot(kc, qt[h])
            if masked:
                key = lax.broadcasted_iota(jnp.int32, s.shape, 0)
                pos = lax.broadcasted_iota(jnp.int32, s.shape, 1) + y * 256
                s = jnp.where(key <= pos, s, -jnp.inf)
            sb[h % 2] = s
            return jnp.maximum(ms[h], jnp.max(s, axis=0, keepdims=True) * (SCALE * LOG2E))

        top = logits(0)
        for h in range(HEADS):
            ahead = logits(h + 1) if h + 1 < HEADS else None
            dp = dot(vc, gt[h]) - cen[h]
            back = jnp.exp2(ms[h] - top)
            w = jnp.exp2(sb[h % 2] * (SCALE * LOG2E) - top)
            ls[h] = ls[h] * back + jnp.sum(w, axis=0, keepdims=True)
            ds[h] = ds[h] * back + jnp.sum(w * dp, axis=0, keepdims=True)
            pb[h, rows, :] = w.astype(bf16)
            db[h, rows, :] = dp.astype(bf16)
            mb[i, h] = top
            ms[h] = top
            top = ahead

    stats(4 + z, True)

    def vy_ready(*slots):
        for slot in slots:
            drain_if(pend["vy", slot])

    ring(2, ("v", "k"))

    @pl.loop(1, 16)
    def _(o):
        piece_copy(o).wait()

    for half in range(2):
        pend["px", half] = []
        for dx in (2, 1, 3):

            def parts(half=half, dx=dx):
                k = half * 3 + dx - 1
                part = kv.at[:, pl.ds(half * 8, 8), x]
                return part, part, (lax.rem(x + dx, 4) * 2 + y_hi, b), px_s.at[k], px_r.at[k]

            pend["px", half].append(send(("px", half, dx), parts))

    ring(2, ("kb",))
    stats_events = {
        0: (lambda: vy_ready(1, 7),),
        1: (lambda: ring(3),),
        2: (lambda: drain(pend["px", 0]),),
        4: (lambda: ring(4), lambda: vy_ready(2, 6)),
        6: (lambda: drain(pend["px", 1]),),
        7: (lambda: ring(5),),
        8: (lambda: vy_ready(3, 5),),
        10: (lambda: vy_ready(4),),
    }
    prompt_at = {2: 0, 3: 1, 6: 2, 7: 3}
    back_at = {0: 1, 1: 7, 4: 2, 5: 6, 8: 3, 9: 5, 10: 4}

    def lookup(table, n, other):
        value = other
        for k, v in table.items():
            value = jnp.where(n == k, v, value)
        return value

    def play(events, n):
        for k, acts in events.items():

            @pl.when(n == k)
            def _():
                for act in acts:
                    act()

    @pl.loop(0, 11)
    def _(n):
        play(stats_events, n)
        chunk = lookup(prompt_at, n, 4 + z - lookup(back_at, n, 0))

        @pl.when((chunk >= 4) | (lookup(prompt_at, n, -1) >= 0))
        def _():
            stats(chunk, False)

    for h in range(HEADS):
        inv = 1.0 / ls[h]
        ls[h] = inv
        ds[h] = ds[h] * inv

    def grads(i):
        rows = aligned(i * KC, KC)
        kt = ks[aligned(i * 4, 4)].reshape(KC, D).T
        dk = jnp.zeros((KC, D), f32)
        dv = jnp.zeros((KC, D), f32)
        for h in range(HEADS):
            w = pb[h, rows, :].astype(f32) * (jnp.exp2(mb[i, h] - ms[h]) * ls[h])
            d_logit = (w * (db[h, rows, :].astype(f32) - ds[h])).astype(bf16)
            sd[h] = d_logit
            dk = dk + dot(d_logit, qh[h])
            dv = dv + dot(w.astype(bf16), gh[h])
        for h in range(HEADS):
            dqt[h] += dot(kt, sd[h])
        return (dk * SCALE).astype(bf16), dv.astype(bf16)

    kz, vz, vy = {}, {}, {}
    xc = []

    def target(way, far):
        return mod8(z + far) if way == 0 else mod8(z - far)

    def sends(way, step, zz):
        ahead = zz + 5 - step
        return (ahead >= 8) | (ahead <= 3) if way == 0 else zz >= 5 - step

    def receives(way, step):
        return sends(way, step, mod8(z - 1) if way == 0 else mod8(z + 1))

    def sees(slot):
        return mod8(z + slot) <= z

    def send_vy(slot):
        def parts():
            return dvr.at[mod8(z + slot), 1 - y], v_y.at[slot], yn, rvy_s.at[slot], rvy_r.at[slot]

        vy[slot] = send_if(("rvy", slot), lambda: sees(slot), parts)

    def wait_vy(slot, ref_index):
        @pl.when(sees(slot))
        def _():
            vy[slot].wait_recv()
            add(dvr, ref_index, v_y[slot])

    def x_send(half):
        for dx in (2, 1, 3):

            def parts(dx=dx):
                k = half * 3 + dx - 1
                span = pl.ds(half * 8, 8)
                xx = lax.rem(x + dx, 4)
                return dp_kv.at[:, span, xx], x_in.at[dx - 1, :, span], (xx * 2 + y_hi, b), x_s.at[k], x_r.at[k]

            xc.append(send(("x", half, dx), parts))

    def add(ref, index, *terms):
        total = ref[index].astype(f32)
        for term in terms:
            total = total + term.astype(f32)
        ref[index] = total.astype(bf16)

    k_lines = (1 - y, y)

    def k_step(step):
        for stream, line in enumerate(k_lines):
            for way, to in ways:
                t = target(way, 5 - step)
                half = pl.ds(way * 128, 128)

                def parts(stream=stream, line=line, way=way, to=to, half=half):
                    t = target(way, 5 - step)
                    k = stream * 8 + way * 4 + step - 1
                    src, dst = dkr.at[t, line], k_in.at[stream, way, step - 1]
                    if step == 1:
                        src, dst = dkr.at[t, line, half], k_in.at[stream, way, 0, half]
                    return src, dst, to, rkz_s.at[k], rkz_r.at[k]

                if step > 1:

                    @pl.when(receives(way, step - 1))
                    def _():
                        kz[stream, way, step - 1].wait_recv()
                        if step == 2:
                            add(dkr, (t, line, half), k_in[stream, way, 0, half])
                        else:
                            add(dkr, (t, line), k_in[stream, way, step - 2])

                kz[stream, way, step] = send_if(
                    ("rkz", stream, way, step), lambda way=way: sends(way, step, z), parts
                )

    def v_step(step):
        far = 5 - step
        if step == 1:
            wait_vy(4, (mod8(z + 4), y))
        for way, to in ways:
            t = target(way, far)
            half = pl.ds(way * 128, 128)

            def parts(way=way, to=to, half=half):
                t = target(way, far)
                k = way * 4 + step - 1
                src, dst = dvr.at[t, y], v_in.at[way, step - 1]
                if step == 1:
                    src, dst = dvr.at[t, y, half], v_in.at[way, 0, half]
                return src, dst, to, rvz_s.at[k], rvz_r.at[k]

            if step > 1:
                wait_vy(far if way == 0 else 8 - far, (t, y))

                @pl.when(receives(way, step - 1))
                def _():
                    vz[way, step - 1].wait_recv()
                    if step == 2:
                        add(dvr, (t, y, half), v_in[way, 0, half])
                    else:
                        add(dvr, (t, y), v_in[way, step - 2])

            vz[way, step] = send_if(("rvz", way, step), lambda way=way: sends(way, step, z), parts)

    def yz_copy(o):
        yh, zz, yl = yz_peer(o)
        return pltpu.make_async_remote_copy(
            src_ref=xs.at[:, zz * 2 + yl, aligned(yh * 16, 16), :],
            dst_ref=yz_in.at[o],
            send_sem=yz_s.at[o],
            recv_sem=yz_r.at[o],
            device_id=(x * 2 + yh, zz * 4 + yl * 2 + c),
            device_id_type=MESH,
        )

    def yz_send():
        for copy in xc:
            copy.wait_recv()
        for i in range(2):
            xs[i] = (
                dp_kv[i, :, x].astype(f32) + x_in[0, i].astype(f32) + x_in[1, i].astype(f32) + x_in[2, i].astype(f32)
            ).astype(bf16)

        @pl.loop(1, 32)
        def _(o):
            yz_copy(1 + lax.rem(o + 6, 31)).start()

    def both(far):
        send_vy(far)
        send_vy(8 - far)

    grads_events = {
        1: (lambda: k_step(1), lambda: send_vy(4)),
        3: (lambda: x_send(0),),
        4: (lambda: v_step(1),),
        5: (lambda: both(3), lambda: k_step(2)),
        7: (lambda: x_send(1),),
        8: (lambda: v_step(2),),
        9: (lambda: both(2), lambda: k_step(3)),
        11: (lambda: both(1), lambda: v_step(3)),
    }
    ahead_at = {0: 4, 3: 3, 4: 5, 7: 2, 8: 6, 9: 1, 10: 7, 11: 0}
    prompt_now = {1: 0, 2: 1, 5: 2, 6: 3}

    @pl.loop(0, 12)
    def _(n):
        play(grads_events, n)
        t = mod8(z + lookup(ahead_at, n, 0))
        is_prompt = lookup(prompt_now, n, -1) >= 0

        @pl.when(is_prompt | (t <= z))
        def _():
            chunk = lookup(prompt_now, n, 4 + t)
            dk, dv = grads(chunk)

            @pl.when(is_prompt)
            def _():
                dp_kv[0, pl.ds(chunk * 4, 4)] = dk.reshape(4, 4, 32, D)
                dp_kv[1, pl.ds(chunk * 4, 4)] = dv.reshape(4, 4, 32, D)

            @pl.when(jnp.logical_not(is_prompt))
            def _():
                dkr[t] = dk.reshape(2, 256, D)
                dvr[t] = dv.reshape(2, 256, D)

    send_vy(0)

    yz_send()
    k_step(4)
    v_step(4)

    dq_copies = []
    for h in range(HEADS):
        dqs[h] = (dqt[h].T * SCALE).astype(bf16)
        to = gq.at[:, aligned(c * 896 + h * D, D)]
        mine = pltpu.make_async_copy(dqs.at[h, aligned(c * 128, 128), :], to, dq_own.at[h])
        mine.start()
        theirs = send(
            ("dq", h),
            lambda h=h, to=to: (dqs.at[h, aligned((1 - c) * 128, 128), :], to, sib, dq_s.at[h], dq_r.at[h]),
        )
        dq_copies.append((mine, theirs))

    yz_in[0] = xs[:, p, aligned(y_hi * 16, 16), :]

    @pl.loop(1, 32)
    def _(o):
        yz_copy(o).wait()

    g_out[...] = jnp.sum(yz_in[...].astype(f32), axis=0).astype(bf16)
    core = r // 4
    part = lax.rem(r, 4)
    for o in range(8):
        dst = pgkv.at[:, aligned(part * 16, 16), aligned(c * 128, 128)]
        s_sem, r_sem = g_s.at[o], g_r.at[part * 2 + c]
        to = (lax.rem(r + o, 8), p * 2 + core)
        if o == 0:

            @pl.when(core == c)
            def _():
                pltpu.make_async_copy(g_out, dst, r_sem).start()

            @pl.when(core != c)
            def _():
                pltpu.make_async_remote_copy(
                    src_ref=g_out, dst_ref=dst, send_sem=s_sem, recv_sem=r_sem, device_id=to, device_id_type=MESH
                ).start()
        else:
            send(("g", o), lambda a=(g_out, dst, to, s_sem, r_sem): a)

    def last_terms(copies, ref, index, ins):
        for way in (0, 1):

            @pl.when(receives(way, 4))
            def _():
                copies(way).wait_recv()
                add(ref, index, ins(way))

    last_terms(lambda way: kz[0, way, 4], dkr, (z, 1 - y), lambda way: k_in[0, way, 3])
    ky_out[...] = dkr[z, 1 - y]
    ky = send(("rky",), lambda: (ky_out, ky_in, yn, rky_s, rky_r))

    last = []

    def finish(i, out):
        to = out.at[:, aligned(c * 128, 128)]
        mine = pltpu.make_async_copy(fin.at[i, aligned(c * 128, 128), :], to, f_sem.at[i])
        mine.start()
        theirs = send(
            ("fin", i),
            lambda: (fin.at[i, aligned((1 - c) * 128, 128), :], to, sib, f_sem.at[2 + i], f_sem.at[4 + i]),
        )
        last.append((mine, theirs))

    wait_vy(0, (z, y))
    last_terms(lambda way: vz[way, 4], dvr, (z, y), lambda way: v_in[way, 3])
    fin[1] = dvr[z, y]
    finish(1, gkv.at[1])
    last_terms(lambda way: kz[1, way, 4], dkr, (z, y), lambda way: k_in[1, way, 3])
    ky.wait_recv()
    fin[0] = (dkr[z, y].astype(f32) + ky_in[...].astype(f32)).astype(bf16)
    finish(0, gkv.at[0])
    for mine, theirs in last + dq_copies:
        mine.wait()
        theirs.wait_recv()
    for k in range(8):
        pltpu.make_async_copy(g_out, pgkv.at[:, 0:16, 0:128], g_r.at[k]).wait()

    @pl.when(core != c)
    def _():
        pltpu.make_async_copy(g_out, pgkv.at[:, 0:16, 0:128], g_s.at[0]).wait()

    for copy in sent.values():
        copy.wait_send()
    for condition, copy in maybe_sent.values():
        pl.when(condition())(copy.wait_send)


def hand_on_kernel(gq, gkv, pgkv, out_q, out_k, out_v, out_pk, out_pv, *held_and_sems):
    held, sems = held_and_sems[:5], held_and_sems[5]
    ins = (gq, gkv.at[0], gkv.at[1], pgkv.at[0], pgkv.at[1])
    outs = (out_q, out_k, out_v, out_pk, out_pv)
    loads = [pltpu.make_async_copy(ins[i], held[i], sems.at[i]) for i in range(5)]
    stores = [pltpu.make_async_copy(held[i], outs[i], sems.at[5 + i]) for i in range(5)]
    for copy in loads:
        copy.start()
    for load, store in zip(loads, stores):
        load.wait()
        store.start()
    for copy in stores:
        copy.wait()


def shards(q, rk, rv, pk, pv, go, lengths):
    rows = q.shape[1]
    dma = pltpu.SemaphoreType.DMA
    n_keys = PROMPT + RESP

    def out(*shape):
        return jax.ShapeDtypeStruct(shape, bf16)

    def v(*shape, dtype=bf16):
        return pltpu.VMEM(shape, dtype)

    def w(*shape):
        return pltpu.VMEM(shape, f32)

    outs = pl.pallas_call(
        fused_kernel,
        out_shape=(out(rows, 1792), out(2, rows, 256), out(2, 64, 256)),
        in_specs=[SMEM] + [ANY] * 6,
        out_specs=(ANY,) * 3,
        scratch_shapes=[
            v(HEADS, 256, D), v(HEADS, 256, D), v(HEADS, D, 256), v(HEADS, D, 256),
            v(2, n_keys // 128, 4, 32, D), v(2, 4, 32, D),
            v(HEADS, n_keys, 256), v(HEADS, n_keys, 256), w(n_keys // KC, HEADS, 1, 256),
            w(HEADS, 1, 256), w(HEADS, 1, 256), w(HEADS, 1, 256), w(HEADS, 1, 256),
            w(2, KC, 256), v(HEADS, KC, 256), w(HEADS, D, 256), v(HEADS, 256, D),
            v(8, 2, 256, D), v(8, 2, 256, D), v(2, 16, 4, 32, D),
            v(2, 2, 4, 256, D), v(2, 4, 256, D), v(8, 256, D), v(256, D), v(256, D), v(2, 256, D),
            v(3, 2, 16, 32, D), v(2, 16, 32, D), v(32, 2, 16, D), v(2, 16, D),
            dma((4,)), dma((4,)), dma((4,)), dma((14,)), dma((14,)), dma((14,)),
            dma((1,)), dma((1,)), dma((24,)), dma((24,)), dma((8,)), dma((8,)),
            dma((16,)), dma((16,)), dma((6,)), dma((6,)),
            dma((16,)), dma((16,)), dma((8,)), dma((8,)), dma((8,)), dma((8,)), dma, dma, dma((6,)),
            dma((6,)), dma((6,)), dma((32,)), dma((32,)), dma((8,)), dma((8,)), dma((7,)), dma((7,)), dma((7,)),
        ],
        compiler_params=pltpu.CompilerParams(
            collective_id=0, has_side_effects=True, vmem_limit_bytes=63 * 2**20
        ),
        name="fused",
    )(
        lengths, q[0], go[0], rk[0].reshape(4, 32, 256), rv[0].reshape(4, 32, 256),
        pk.reshape(2, 32, 256), pv.reshape(2, 32, 256),
    )
    results = ((rows, 1792), (rows, 256), (rows, 256), (64, 256), (64, 256))
    gq, gk, gv, pkg, pvg = pl.pallas_call(
        hand_on_kernel,
        out_shape=tuple(out(*shape) for shape in results),
        in_specs=[ANY] * 3,
        out_specs=(ANY,) * 5,
        scratch_shapes=[v(*shape) for shape in results] + [dma((10,))],
        compiler_params=pltpu.CompilerParams(vmem_limit_bytes=63 * 2**20),
        name="hand_on",
    )(*outs)
    return gq[None], gk[None], gv[None], pkg, pvg


def solution(mesh):
    in_specs = (
        P("resp", "blk", None),
        P("resp", "blk", None),
        P("resp", "blk", None),
        P("blk", None),
        P("blk", None),
        P("resp", "blk", None),
        P("resp"),
    )
    out_specs = (
        P("resp", "blk", None),
        P("resp", "blk", None),
        P("resp", "blk", None),
        P("blk", None),
        P("blk", None),
    )
    return jax.shard_map(shards, mesh=mesh, in_specs=in_specs, out_specs=out_specs, check_vma=False)
```
